128 devices in a mesh: sub: 16 (over z, y), col: 8 (over x, core).
Axes of the slice: x: 4, y: 4, z: 4, core: 2. Of those that a mesh axis runs over, the one named last changes fastest.
Arguments:
- z_basis: bfloat16 [32, 16, 6, 64, 4096], P('sub', 'col'), may hold values from -6 to 6
- jac_center: bfloat16 [32, 16, 6, 6, 4096], P('sub', 'col'), may hold values from -0.0234375 to 0.0234375
- jac_lower: bfloat16 [32, 16, 6, 6, 4096], P('sub', 'col'), may hold values from -0.0234375 to 0.0234375
- jac_upper: bfloat16 [32, 16, 6, 6, 4096], P('sub', 'col'), may hold values from -0.0234375 to 0.0234375
- face_cells: int32 [32, 16, 4, 128], P('sub', 'col'), may hold values from 0 to 4095
- couple: bfloat16 [32, 16, 4, 6, 6, 128], P('sub', 'col'), may hold values from -0.21875 to 0.21875
Outputs:
- diag_tiles: float32 [32, 16, 64, 64], P('sub', 'col')
- off_tiles: float32 [32, 16, 4, 64, 64], P('sub', 'col')
The draws below stay inside these ranges and needn't reach their ends.
All inputs are finite; a program needn't handle non-finite values.
Results may differ from the reference program's by a relative error of at most 0.0029.
Values may be sent and summed in bfloat16 or wider, within the bound.
A program may use at most 192 MiB of HBM per device.

```python
import jax
import jax.numpy as jnp
from jax import lax

K = 64
COMP = 6
CELLS = 4096
FACE = 128
GX = 32
GY = 16


def with_ends(drawn, key, smallest, high):
    index_at = [jax.random.randint(jax.random.fold_in(key, axis), (), 0, length) for axis, length in enumerate(drawn.shape)]
    longest = drawn.shape.index(max(drawn.shape))
    beside = index_at[:longest] + [(index_at[longest] + 1) % drawn.shape[longest]] + index_at[longest + 1:]
    return drawn.at[tuple(index_at)].set(smallest).at[tuple(beside)].set(high)


def block_levels(stream_key, dims, pieces, least, high):
    factor_of, own = 1.0, jax.random.fold_in(stream_key, 6)
    for dim, shards_of in pieces:
        draws = jnp.exp(jax.random.uniform(jax.random.fold_in(own, dim), (shards_of,), jnp.float32, least / len(pieces), high / len(pieces)))
        factor_of = factor_of * jnp.repeat(draws, dims[dim] // shards_of).reshape([-1 if axis == dim else 1 for axis in range(len(dims))])
    return factor_of


def bell_draw(rng, shape, spread, most, cuts=(), kind=jnp.bfloat16):
    loudness = block_levels(rng, shape, cuts, -0.22, 0.18) if cuts else 1.0
    values = jax.random.normal(rng, shape, jnp.float32) * spread * loudness
    return jnp.minimum(jnp.maximum(values, -most), most).astype(kind)


def setup_inputs(seed: int = 0) -> dict:
    key_of = jax.random.split(jax.random.key(seed), 7)
    return {
        "z_basis": bell_draw(key_of[0], (GX, GY, COMP, K, CELLS), 1.0, 6.0, ((0, 16), (1, 8))),
        "jac_center": bell_draw(key_of[1], (GX, GY, COMP, COMP, CELLS), (18 * CELLS) ** -0.5, 0.0234375, ((0, 16), (1, 8))),
        "jac_lower": bell_draw(key_of[2], (GX, GY, COMP, COMP, CELLS), (18 * CELLS) ** -0.5, 0.0234375, ((0, 16), (1, 8))),
        "jac_upper": bell_draw(key_of[3], (GX, GY, COMP, COMP, CELLS), (18 * CELLS) ** -0.5, 0.0234375, ((0, 16), (1, 8))),
        "face_cells": with_ends(jax.random.randint(key_of[4], (GX, GY, 4, FACE), 0, CELLS), jax.random.fold_in(key_of[4], 1), 0, CELLS - 1).astype(jnp.int32),
        "couple": bell_draw(key_of[5], (GX, GY, 4, COMP, COMP, FACE), (6 * FACE) ** -0.5, 0.21875, ((0, 16), (1, 8))),
    }


OPPOSITE = (1, 0, 3, 2)


def apply_jacobian(vectors, center, lower, upper):
    values = vectors.astype(jnp.float32)
    zeros_edge = jnp.zeros_like(values[..., :1])
    before = jnp.concatenate([zeros_edge, values[..., :-1]], axis=-1)
    after = jnp.concatenate([values[..., 1:], zeros_edge], axis=-1)
    total = jnp.einsum("yabc,ybkc->yakc", center.astype(jnp.float32), values)
    total = total + jnp.einsum("yabc,ybkc->yakc", lower.astype(jnp.float32), before)
    total = total + jnp.einsum("yabc,ybkc->yakc", upper.astype(jnp.float32), after)
    return total.astype(jnp.bfloat16)


def push_faces(weights, faces):
    total = jnp.einsum("xyabh,xybkh->xyakh", weights.astype(jnp.float32), faces.astype(jnp.float32))
    return total.astype(jnp.bfloat16)


def diagonal_row(operands):
    vectors, center, lower, upper = operands
    applied = apply_jacobian(vectors, center, lower, upper)
    return jnp.einsum("yakc,yalc->ykl", vectors.astype(jnp.float32), applied.astype(jnp.float32))


def face_values(vectors, cells):
    return jax.vmap(jax.vmap(lambda source, picked: jnp.take(source, picked, axis=2)))(vectors, cells)


def neighbour(values, facing):
    padded = jnp.pad(values, [(1, 1), (1, 1)] + [(0, 0)] * (values.ndim - 2))
    if facing == 0:
        return padded[2:, 1:-1]
    if facing == 1:
        return padded[:-2, 1:-1]
    if facing == 2:
        return padded[1:-1, 2:]
    return padded[1:-1, :-2]


def reference(z_basis, jac_center, jac_lower, jac_upper, face_cells, couple):
    diag_tiles = lax.map(diagonal_row, (z_basis, jac_center, jac_lower, jac_upper))
    tiles = []
    for facing in range(4):
        back = OPPOSITE[facing]
        own = face_values(z_basis, face_cells[:, :, facing])
        pushed = push_faces(couple[:, :, back], face_values(z_basis, face_cells[:, :, back]))
        arrived = neighbour(pushed, facing)
        tiles.append(jnp.einsum("xyakh,xyalh->xykl", own.astype(jnp.float32), arrived.astype(jnp.float32)))
    off_tiles = jnp.stack(tiles, axis=2)
    return diag_tiles, off_tiles
```

```python
import functools

import jax
import jax.numpy as jnp
from jax import lax
from jax.experimental import pallas as pl
from jax.experimental.pallas import tpu as pltpu
from jax.sharding import PartitionSpec as P

MESH = pl.DeviceIdType.MESH
F32 = jnp.float32
BF16 = jnp.bfloat16
NT = (((1,), (1,)), ((), ()))
ROWS = 8
LANES = 128
WIDE = 256
PIECE = 512
OPPOSITE = (1, 0, 3, 2)


def neighbour_of(facing):
    sub, col = lax.axis_index("sub"), lax.axis_index("col")
    subs, cols = lax.axis_size("sub"), lax.axis_size("col")
    if facing == 0:
        return lax.rem(sub + 1, subs), col
    if facing == 1:
        return lax.rem(sub + subs - 1, subs), col
    if facing == 2:
        return sub, lax.rem(col + 1, cols)
    return sub, lax.rem(col + cols - 1, cols)


def has_neighbour(facing):
    sub, col = lax.axis_index("sub"), lax.axis_index("col")
    if facing == 0:
        return sub < lax.axis_size("sub") - 1
    if facing == 1:
        return sub > 0
    if facing == 2:
        return col < lax.axis_size("col") - 1
    return col > 0


def kernel(dims, z_hbm, jc_hbm, jl_hbm, ju_hbm, cells_ref, couple_ref, diag_ref, off_ref,
           z, jac, coef, applied, gather, faces, pushed, arrived, load_sem, send_sem, recv_sem):
    nx, ny, comp, kdim, ncell, nface = dims
    subs = nx * ny
    chunks = ncell // WIDE
    tiles = [(t, k0) for t in range(WIDE // LANES) for k0 in range(0, kdim, ROWS)]

    def loads(s):
        pairs = [(z_hbm.at[s], z.at[s])]
        pairs += [(ref.at[s], jac.at[s, n]) for n, ref in enumerate((jc_hbm, jl_hbm, ju_hbm))]
        return [pltpu.make_async_copy(src, dst, load_sem.at[s, n]) for n, (src, dst) in enumerate(pairs)]

    for s in range(subs):
        for copy in loads(s):
            copy.start()
    barrier = pltpu.get_barrier_semaphore()
    for facing in range(4):
        pl.semaphore_signal(barrier, inc=1, device_id=neighbour_of(facing), device_id_type=MESH)

    diag_ref[...] = jnp.zeros_like(diag_ref)
    applied[1] = jnp.zeros_like(applied[1])

    lane = lax.broadcasted_iota(jnp.int32, (ROWS, LANES), 1)
    first, last = lane == 0, lane == LANES - 1

    def chunk(n, side, extra):
        s = n // chunks
        c0 = pl.multiple_of(lax.rem(n, chunks) * WIDE, WIDE)
        cell = lax.broadcasted_iota(jnp.int32, (comp, WIDE), 1) + c0
        for a in range(comp):
            for d in range(3):
                block = jac[s, d, a, :, pl.ds(c0, WIDE)].astype(F32)
                if d == 1:
                    block = jnp.where(cell == 0, 0.0, block)
                if d == 2:
                    block = jnp.where(cell == ncell - 1, 0.0, block)
                coef[side, d * comp + a, 0:comp] = block
        past = jnp.maximum(n - 1, 0)
        sp = past // chunks
        cq = pl.multiple_of(lax.rem(past, chunks) * WIDE, WIDE)
        total = []

        def tile_dot(a):
            total.append(
                lax.dot_general(
                    applied[1 - side, a], z[sp, a, :, pl.ds(cq, WIDE)], NT, preferred_element_type=F32
                )
            )

        slots = {}
        for a in range(comp):
            slots.setdefault(a * len(tiles) // comp, []).append(functools.partial(tile_dot, a))
        for m, step in enumerate(extra):
            slots.setdefault((2 * m + 1) * len(tiles) // (2 * len(extra)), []).append(step)

        for m, (t, k0) in enumerate(tiles):
            for step in slots.get(m, []):
                step()
            cc = pl.multiple_of(c0 + t * LANES, LANES)
            cm = pl.multiple_of(jnp.maximum(cc - LANES, 0), LANES)
            cp = pl.multiple_of(jnp.minimum(cc + LANES, ncell - LANES), LANES)
            values = []
            for b in range(comp):
                here = z[s, b, k0 : k0 + ROWS, pl.ds(cc, LANES)]
                low = jnp.where(last, z[s, b, k0 : k0 + ROWS, pl.ds(cm, LANES)], here)
                high = jnp.where(first, z[s, b, k0 : k0 + ROWS, pl.ds(cp, LANES)], here)
                values.append(
                    (
                        here.astype(F32),
                        pltpu.roll(low.astype(F32), 1, 1),
                        pltpu.roll(high.astype(F32), LANES - 1, 1),
                    )
                )
            for a in range(comp):
                acc = None
                for b in range(comp):
                    for d in range(3):
                        weight = coef[side, d * comp + a, b : b + 1, t * LANES : (t + 1) * LANES]
                        term = weight * values[b][d]
                        acc = term if acc is None else acc + term
                applied[side, a, k0 : k0 + ROWS, t * LANES : (t + 1) * LANES] = acc.astype(BF16)
        diag_ref[sp] += functools.reduce(lambda p, q: p + q, total)

    def with_faces(it, carry):
        for s in range(1, subs):
            @pl.when(it == s * 4)
            def _():
                for copy in loads(s):
                    copy.wait()

        fs = it // 4
        pair = lax.rem(it, 4) // 2
        half = lax.rem(it, 2)
        wanted = jnp.concatenate(
            [cells_ref[fs, pl.ds(2 * pair, 1)], cells_ref[fs, pl.ds(2 * pair + 1, 1)]], axis=1
        )

        def piece(h):
            k0 = pl.multiple_of(half * (ncell // 2) + h * PIECE, PIECE)
            position = lax.broadcasted_iota(jnp.int32, (PIECE, 2 * nface), 0)
            pick = jnp.where(position == wanted - k0, 1.0, 0.0).astype(BF16)
            part = jnp.dot(
                z[fs, :, :, pl.ds(k0, PIECE)].reshape(comp * kdim, PIECE), pick, preferred_element_type=F32
            )
            if h == 0:
                part = part + jnp.where(half == 0, 0.0, gather[...])
            else:
                part = part + gather[...]
            gather[...] = part
            if h == ncell // 2 // PIECE - 1:
                for b in range(comp):
                    for e in range(2):
                        faces[fs, 2 * pair + e, :, b * nface : (b + 1) * nface] = part[
                            b * kdim : (b + 1) * kdim, e * nface : (e + 1) * nface
                        ].astype(BF16)

        steps = [functools.partial(piece, h) for h in range(ncell // 2 // PIECE)]
        chunk(2 * it, 0, steps[: len(steps) // 2])
        chunk(2 * it + 1, 1, steps[len(steps) // 2 :])
        return carry

    def without_faces(it, carry):
        chunk(2 * it, 0, [])
        chunk(2 * it + 1, 1, [])
        return carry

    for copy in loads(0):
        copy.wait()
    half_way = subs * chunks // 4
    lax.fori_loop(0, half_way, with_faces, 0)

    def push(q, carry):
        s, d = q // 4, lax.rem(q, 4)
        picked = [faces[s, d, :, b * nface : (b + 1) * nface].astype(F32) for b in range(comp)]
        for a in range(comp):
            weights = couple_ref[s, d, a].astype(F32)
            acc = None
            for b in range(comp):
                term = weights[b : b + 1] * picked[b]
                acc = term if acc is None else acc + term
            pushed[s, d, :, a * nface : (a + 1) * nface] = acc.astype(BF16)
        return carry

    lax.fori_loop(0, subs * 4, push, 0)

    pl.semaphore_wait(barrier, 4)

    def sources(d):
        if d == 0:
            return [(nx - 1) * ny + j for j in range(ny)]
        if d == 1:
            return list(range(ny))
        if d == 2:
            return [i * ny + ny - 1 for i in range(nx)]
        return [i * ny for i in range(nx)]

    sends = []
    for d in range(4):
        for m, s in enumerate(sources(d)):
            sends.append(
                pltpu.make_async_remote_copy(
                    src_ref=pushed.at[s, d],
                    dst_ref=arrived.at[d, m],
                    send_sem=send_sem.at[d, m],
                    recv_sem=recv_sem.at[d, m],
                    device_id=neighbour_of(d),
                    device_id_type=MESH,
                )
            )
    for copy in sends:
        copy.start()

    lax.fori_loop(half_way, 2 * half_way, without_faces, 0)

    final = functools.reduce(
        lambda p, q: p + q,
        [
            lax.dot_general(applied[1, a], z[subs - 1, a, :, ncell - WIDE :], NT, preferred_element_type=F32)
            for a in range(comp)
        ],
    )
    diag_ref[subs - 1] += final
    for s in range(subs):
        diag_ref[s] = diag_ref[s].T

    def tile(s, e, right):
        return lax.dot_general(faces[s, e], right, NT, preferred_element_type=F32)

    steps_of = ((1, 0), (-1, 0), (0, 1), (0, -1))
    for i in range(nx):
        for j in range(ny):
            for e in range(4):
                ti, tj = i + steps_of[e][0], j + steps_of[e][1]
                if 0 <= ti < nx and 0 <= tj < ny:
                    off_ref[i * ny + j, e] = tile(i * ny + j, e, pushed[ti * ny + tj, OPPOSITE[e]])
    for copy in sends:
        copy.wait()
    for e in range(4):
        d = OPPOSITE[e]
        inside = has_neighbour(e)
        for m, s in enumerate(sources(e)):
            off_ref[s, e] = jnp.where(inside, tile(s, e, arrived[d, m]), 0.0)


def on_device(z_basis, jac_center, jac_lower, jac_upper, face_cells, couple):
    nx, ny, comp, kdim, ncell = z_basis.shape
    nface = face_cells.shape[-1]
    subs = nx * ny
    rank = lambda array: array.reshape((subs,) + array.shape[2:])
    wide = comp * nface
    diag, off = pl.pallas_call(
        functools.partial(kernel, (nx, ny, comp, kdim, ncell, nface)),
        out_shape=(
            jax.ShapeDtypeStruct((subs, kdim, kdim), F32),
            jax.ShapeDtypeStruct((subs, 4, kdim, kdim), F32),
        ),
        in_specs=[pl.BlockSpec(memory_space=pl.ANY)] * 4 + [pl.BlockSpec(memory_space=pltpu.VMEM)] * 2,
        out_specs=[pl.BlockSpec(memory_space=pltpu.VMEM)] * 2,
        scratch_shapes=[
            pltpu.VMEM((subs, comp, kdim, ncell), BF16),
            pltpu.VMEM((subs, 3, comp, comp, ncell), BF16),
            pltpu.VMEM((2, 3 * comp, 8, WIDE), F32),
            pltpu.VMEM((2, comp, kdim, WIDE), BF16),
            pltpu.VMEM((comp * kdim, 2 * nface), F32),
            pltpu.VMEM((subs, 4, kdim, wide), BF16),
            pltpu.VMEM((subs, 4, kdim, wide), BF16),
            pltpu.VMEM((4, 2, kdim, wide), BF16),
            pltpu.SemaphoreType.DMA((subs, 4)),
            pltpu.SemaphoreType.DMA((4, 2)),
            pltpu.SemaphoreType.DMA((4, 2)),
        ],
        compiler_params=pltpu.CompilerParams(
            collective_id=0, has_side_effects=True, vmem_limit_bytes=56 * 2**20
        ),
        cost_estimate=pl.CostEstimate(flops=10**10, bytes_accessed=17 * 10**6, transcendentals=0),
    )(*(rank(x) for x in (z_basis, jac_center, jac_lower, jac_upper, face_cells, couple)))
    return diag.reshape(nx, ny, kdim, kdim), off.reshape(nx, ny, 4, kdim, kdim)


def solution(mesh):
    in_specs = (
        P("sub", "col", None, None, None),
        P("sub", "col", None, None, None),
        P("sub", "col", None, None, None),
        P("sub", "col", None, None, None),
        P("sub", "col", None, None),
        P("sub", "col", None, None, None, None),
    )
    out_specs = (P("sub", "col", None, None), P("sub", "col", None, None, None))
    return jax.shard_map(
        on_device, mesh=mesh, in_specs=in_specs, out_specs=out_specs, check_vma=False
    )
```

```python
import functools

import jax
import jax.numpy as jnp
from jax import lax
from jax.experimental import pallas as pl
from jax.experimental.pallas import tpu as pltpu
from jax.sharding import PartitionSpec as P

MESH = pl.DeviceIdType.MESH
F32 = jnp.float32
BF16 = jnp.bfloat16
NT = (((1,), (1,)), ((), ()))
ROWS = 8
LANES = 128
WIDE = 256
PIECE = 512
OPPOSITE = (1, 0, 3, 2)


def neighbour_of(facing):
    sub, col = lax.axis_index("sub"), lax.axis_index("col")
    subs, cols = lax.axis_size("sub"), lax.axis_size("col")
    if facing == 0:
        return lax.rem(sub + 1, subs), col
    if facing == 1:
        return lax.rem(sub + subs - 1, subs), col
    if facing == 2:
        return sub, lax.rem(col + 1, cols)
    return sub, lax.rem(col + cols - 1, cols)


def has_neighbour(facing):
    sub, col = lax.axis_index("sub"), lax.axis_index("col")
    if facing == 0:
        return sub < lax.axis_size("sub") - 1
    if facing == 1:
        return sub > 0
    if facing == 2:
        return col < lax.axis_size("col") - 1
    return col > 0


def kernel(dims, z_hbm, jc_hbm, jl_hbm, ju_hbm, cells_ref, couple_ref, diag_ref, off_ref,
           z, jac, coef, applied, gather, faces, pushed, arrived, load_sem, send_sem, recv_sem):
    nx, ny, comp, kdim, ncell, nface = dims
    subs = nx * ny
    chunks = ncell // WIDE
    quarter = ncell // 4
    tiles = [(t, k0) for t in range(WIDE // LANES) for k0 in range(0, kdim, ROWS)]

    def loads(n):
        i, at = n // 4, pl.multiple_of(lax.rem(n, 4) * quarter, quarter)
        pairs = [
            (z_hbm.at[i * ny + j, :, :, pl.ds(at, quarter)], z.at[i * ny + j, :, :, pl.ds(LANES + at, quarter)])
            for j in range(ny)
        ]
        pairs += [
            (ref.at[i, :, :, :, pl.ds(at, quarter)], jac.at[m, i, :, :, :, pl.ds(at, quarter)])
            for m, ref in enumerate((jc_hbm, jl_hbm, ju_hbm))
        ]
        return [pltpu.make_async_copy(src, dst, load_sem.at[n, m]) for m, (src, dst) in enumerate(pairs)]

    for n in range(4 * nx):
        for copy in loads(n):
            copy.start()
    barrier = pltpu.get_barrier_semaphore()
    for facing in range(4):
        pl.semaphore_signal(barrier, inc=1, device_id=neighbour_of(facing), device_id_type=MESH)

    diag_ref[...] = jnp.zeros_like(diag_ref)
    applied[1] = jnp.zeros_like(applied[1])
    zero = jnp.zeros((comp, kdim, LANES), BF16)
    for s in range(subs):
        z[s, :, :, 0:LANES] = zero
        z[s, :, :, LANES + ncell :] = zero

    lane = lax.broadcasted_iota(jnp.int32, (ROWS, LANES), 1)
    first, last = lane == 0, lane == LANES - 1

    def stencil(it, side, extra):
        i = it // chunks
        s = i * ny + side
        c0 = pl.multiple_of(lax.rem(it, chunks) * WIDE, WIDE)
        past = it if side else jnp.maximum(it - 1, 0)
        sp = past // chunks * ny + 1 - side
        cq = pl.multiple_of(lax.rem(past, chunks) * WIDE + LANES, LANES)
        total = []

        def tile_dot(a):
            total.append(
                lax.dot_general(
                    applied[1 - side, a], z[sp, a, :, pl.ds(cq, WIDE)], NT, preferred_element_type=F32
                )
            )

        slots = {}
        for a in range(comp):
            slots.setdefault(a * len(tiles) // comp, []).append(functools.partial(tile_dot, a))
        for m, step in enumerate(extra):
            slots.setdefault((2 * m + 1) * len(tiles) // (2 * len(extra)), []).append(step)

        for m, (t, k0) in enumerate(tiles):
            for step in slots.get(m, []):
                step()
            at = pl.multiple_of(c0 + (t + 1) * LANES, LANES)
            values = []
            for b in range(comp):
                here = z[s, b, k0 : k0 + ROWS, pl.ds(at, LANES)]
                low = jnp.where(last, z[s, b, k0 : k0 + ROWS, pl.ds(at - LANES, LANES)], here)
                high = jnp.where(first, z[s, b, k0 : k0 + ROWS, pl.ds(at + LANES, LANES)], here)
                values.append(
                    (
                        here.astype(F32),
                        pltpu.roll(low.astype(F32), 1, 1),
                        pltpu.roll(high.astype(F32), LANES - 1, 1),
                    )
                )
            for a in range(comp):
                acc = None
                for b in range(comp):
                    for d in range(3):
                        weight = coef[d, a, b, side : side + 1, t * LANES : (t + 1) * LANES]
                        term = weight * values[b][d]
                        acc = term if acc is None else acc + term
                applied[side, a, k0 : k0 + ROWS, t * LANES : (t + 1) * LANES] = acc.astype(BF16)
        diag_ref[sp] += functools.reduce(lambda p, q: p + q, total)

    def weights(it):
        i = it // chunks
        c0 = pl.multiple_of(lax.rem(it, chunks) * WIDE, WIDE)
        for d in range(3):
            for a in range(comp):
                coef[d, a] = jac[d, i, a, :, :, pl.ds(c0, WIDE)].astype(F32)

    def with_faces(it, carry):
        @pl.when((lax.rem(it, 2) == 1) & (it < 8 * nx - 1))
        def _():
            for copy in loads((it + 1) // 2):
                copy.wait()

        i = it // 8
        fs = i * ny + lax.rem(it, 2)
        block = lax.rem(it, 8) // 2

        def piece(h):
            pair, k = h % 2, h // 2
            k0 = pl.multiple_of(block * quarter + k * PIECE, PIECE)
            wanted = jnp.concatenate(
                [cells_ref[fs, 2 * pair : 2 * pair + 1], cells_ref[fs, 2 * pair + 1 : 2 * pair + 2]], axis=1
            )
            position = lax.broadcasted_iota(jnp.int32, (PIECE, 2 * nface), 0)
            pick = jnp.where(position == wanted - k0, 1.0, 0.0).astype(BF16)
            part = jnp.dot(
                z[fs, :, :, pl.ds(pl.multiple_of(k0 + LANES, LANES), PIECE)].reshape(comp * kdim, PIECE),
                pick,
                preferred_element_type=F32,
            )
            if k == 0:
                gather[fs, pair] = part + jnp.where(block == 0, 0.0, gather[fs, pair])
            else:
                gather[fs, pair] += part

        steps = [functools.partial(piece, h) for h in range(2 * quarter // PIECE)]
        weights(it)
        stencil(it, 0, steps[: len(steps) // 2])
        stencil(it, 1, steps[len(steps) // 2 :])
        return carry

    def without_faces(it, carry):
        weights(it)
        stencil(it, 0, [])
        stencil(it, 1, [])
        return carry

    for copy in loads(0):
        copy.wait()
    lax.fori_loop(0, 8 * nx, with_faces, 0)

    def push(s, carry):
        for d in range(4):
            picked = []
            for b in range(comp):
                values = gather[s, d // 2, b * kdim : (b + 1) * kdim, (d % 2) * nface : (d % 2 + 1) * nface]
                faces[s, d, :, b * nface : (b + 1) * nface] = values.astype(BF16)
                picked.append(values)
            for a in range(comp):
                acc = None
                for b in range(comp):
                    term = couple_ref[s, a, b].astype(F32)[d : d + 1] * picked[b]
                    acc = term if acc is None else acc + term
                pushed[s, d, :, a * nface : (a + 1) * nface] = acc.astype(BF16)
        return carry

    lax.fori_loop(0, subs, push, 0)

    pl.semaphore_wait(barrier, 4)

    def sources(d):
        if d == 0:
            return [(nx - 1) * ny + j for j in range(ny)]
        if d == 1:
            return list(range(ny))
        if d == 2:
            return [i * ny + ny - 1 for i in range(nx)]
        return [i * ny for i in range(nx)]

    sends = []
    for d in range(4):
        for m, s in enumerate(sources(d)):
            sends.append(
                pltpu.make_async_remote_copy(
                    src_ref=pushed.at[s, d],
                    dst_ref=arrived.at[d, m],
                    send_sem=send_sem.at[d, m],
                    recv_sem=recv_sem.at[d, m],
                    device_id=neighbour_of(d),
                    device_id_type=MESH,
                )
            )
    for copy in sends:
        copy.start()

    lax.fori_loop(8 * nx, nx * chunks, without_faces, 0)

    final = functools.reduce(
        lambda p, q: p + q,
        [
            lax.dot_general(
                applied[1, a], z[subs - 1, a, :, LANES + ncell - WIDE : LANES + ncell], NT,
                preferred_element_type=F32,
            )
            for a in range(comp)
        ],
    )
    diag_ref[subs - 1] += final
    for s in range(subs):
        diag_ref[s] = diag_ref[s].T

    def tile(s, e, right):
        return lax.dot_general(faces[s, e], right, NT, preferred_element_type=F32)

    steps_of = ((1, 0), (-1, 0), (0, 1), (0, -1))
    for i in range(nx):
        for j in range(ny):
            for e in range(4):
                ti, tj = i + steps_of[e][0], j + steps_of[e][1]
                if 0 <= ti < nx and 0 <= tj < ny:
                    off_ref[i * ny + j, e] = tile(i * ny + j, e, pushed[ti * ny + tj, OPPOSITE[e]])
    for copy in sends:
        copy.wait()
    for e in range(4):
        d = OPPOSITE[e]
        inside = has_neighbour(e)
        for m, s in enumerate(sources(e)):
            off_ref[s, e] = jnp.where(inside, tile(s, e, arrived[d, m]), 0.0)


def hand_over(diag_in, off_in, diag_out, off_out, sem):
    copies = [
        pltpu.make_async_copy(src, dst, sem.at[n])
        for n, (src, dst) in enumerate(((diag_in, diag_out), (off_in, off_out)))
    ]
    for copy in copies:
        copy.start()
    for copy in copies:
        copy.wait()


def on_device(z_basis, jac_center, jac_lower, jac_upper, face_cells, couple):
    nx, ny, comp, kdim, ncell = z_basis.shape
    nface = face_cells.shape[-1]
    subs = nx * ny
    merge = lambda array: array.reshape((subs,) + array.shape[2:])
    paired = [jnp.transpose(array, (0, 2, 3, 1, 4)) for array in (jac_center, jac_lower, jac_upper)]
    wide = comp * nface
    shapes = (
        jax.ShapeDtypeStruct((subs, kdim, kdim), F32),
        jax.ShapeDtypeStruct((subs, 4, kdim, kdim), F32),
    )
    results = pl.pallas_call(
        functools.partial(kernel, (nx, ny, comp, kdim, ncell, nface)),
        out_shape=shapes,
        in_specs=[pl.BlockSpec(memory_space=pl.ANY)] * 4 + [pl.BlockSpec(memory_space=pltpu.VMEM)] * 2,
        out_specs=[pl.BlockSpec(memory_space=pltpu.VMEM)] * 2,
        scratch_shapes=[
            pltpu.VMEM((subs, comp, kdim, ncell + 2 * LANES), BF16),
            pltpu.VMEM((3, nx, comp, comp, ny, ncell), BF16),
            pltpu.VMEM((3, comp, comp, ny, WIDE), F32),
            pltpu.VMEM((2, comp, kdim, WIDE), BF16),
            pltpu.VMEM((subs, 2, comp * kdim, 2 * nface), F32),
            pltpu.VMEM((subs, 4, kdim, wide), BF16),
            pltpu.VMEM((subs, 4, kdim, wide), BF16),
            pltpu.VMEM((4, 2, kdim, wide), BF16),
            pltpu.SemaphoreType.DMA((4 * nx, 3 + ny)),
            pltpu.SemaphoreType.DMA((4, 2)),
            pltpu.SemaphoreType.DMA((4, 2)),
        ],
        compiler_params=pltpu.CompilerParams(
            collective_id=0, has_side_effects=True, vmem_limit_bytes=56 * 2**20
        ),
        cost_estimate=pl.CostEstimate(flops=10**10, bytes_accessed=17 * 10**6, transcendentals=0),
    )(
        merge(z_basis), *paired, merge(face_cells), merge(jnp.transpose(couple, (0, 1, 3, 4, 2, 5)))
    )
    diag, off = pl.pallas_call(
        hand_over,
        out_shape=shapes,
        in_specs=[pl.BlockSpec(memory_space=pl.ANY)] * 2,
        out_specs=[pl.BlockSpec(memory_space=pl.ANY)] * 2,
        scratch_shapes=[pltpu.SemaphoreType.DMA((2,))],
        compiler_params=pltpu.CompilerParams(vmem_limit_bytes=56 * 2**20),
    )(*results)
    return diag.reshape(nx, ny, kdim, kdim), off.reshape(nx, ny, 4, kdim, kdim)


def solution(mesh):
    in_specs = (
        P("sub", "col", None, None, None),
        P("sub", "col", None, None, None),
        P("sub", "col", None, None, None),
        P("sub", "col", None, None, None),
        P("sub", "col", None, None),
        P("sub", "col", None, None, None, None),
    )
    out_specs = (P("sub", "col", None, None), P("sub", "col", None, None, None))
    return jax.shard_map(
        on_device, mesh=mesh, in_specs=in_specs, out_specs=out_specs, check_vma=False
    )
```

```python
import functools

import jax
import jax.numpy as jnp
from jax import lax
from jax.experimental import pallas as pl
from jax.experimental.pallas import tpu as pltpu
from jax.sharding import PartitionSpec as P

MESH = pl.DeviceIdType.MESH
F32 = jnp.float32
BF16 = jnp.bfloat16
NT = (((1,), (1,)), ((), ()))
ROWS = 8
LANES = 128
WIDE = 256
PIECE = 512
OPPOSITE = (1, 0, 3, 2)


def neighbour_of(facing):
    sub, col = lax.axis_index("sub"), lax.axis_index("col")
    subs, cols = lax.axis_size("sub"), lax.axis_size("col")
    if facing == 0:
        return lax.rem(sub + 1, subs), col
    if facing == 1:
        return lax.rem(sub + subs - 1, subs), col
    if facing == 2:
        return sub, lax.rem(col + 1, cols)
    return sub, lax.rem(col + cols - 1, cols)


def has_neighbour(facing):
    sub, col = lax.axis_index("sub"), lax.axis_index("col")
    if facing == 0:
        return sub < lax.axis_size("sub") - 1
    if facing == 1:
        return sub > 0
    if facing == 2:
        return col < lax.axis_size("col") - 1
    return col > 0


def kernel(dims, z_hbm, jc_hbm, jl_hbm, ju_hbm, cells_ref, couple_ref, diag_ref, off_ref,
           z, jac, coef, applied, gather, faces, pushed, arrived, load_sem, send_sem, recv_sem):
    nx, ny, comp, kdim, ncell, nface = dims
    subs = nx * ny
    chunks = ncell // WIDE
    quarter = ncell // 4
    all_tiles = [(t, k0) for t in range(WIDE // LANES) for k0 in range(0, kdim, ROWS)]

    def loads(n):
        i, at = n // 4, pl.multiple_of(lax.rem(n, 4) * quarter, quarter)
        pairs = [
            (z_hbm.at[i * ny + j, :, :, pl.ds(at, quarter)], z.at[i * ny + j, :, :, pl.ds(LANES + at, quarter)])
            for j in range(ny)
        ]
        pairs += [
            (ref.at[i, :, :, :, pl.ds(at, quarter)], jac.at[m, i, :, :, :, pl.ds(at, quarter)])
            for m, ref in enumerate((jc_hbm, jl_hbm, ju_hbm))
        ]
        return [pltpu.make_async_copy(src, dst, load_sem.at[n, m]) for m, (src, dst) in enumerate(pairs)]

    for n in range(4 * nx):
        for copy in loads(n):
            copy.start()
    barrier = pltpu.get_barrier_semaphore()
    for facing in range(4):
        pl.semaphore_signal(barrier, inc=1, device_id=neighbour_of(facing), device_id_type=MESH)

    diag_ref[...] = jnp.zeros_like(diag_ref)
    applied[1] = jnp.zeros_like(applied[1])
    zero = jnp.zeros((comp, kdim, LANES), BF16)
    for s in range(subs):
        z[s, :, :, 0:LANES] = zero
        z[s, :, :, LANES + ncell :] = zero

    lane = lax.broadcasted_iota(jnp.int32, (ROWS, LANES), 1)
    first, last = lane == 0, lane == LANES - 1
    place = lax.broadcasted_iota(jnp.int32, (16, 2 * nface), 0).astype(jnp.int16)
    one, nil = jnp.ones((16, 2 * nface), BF16), jnp.zeros((16, 2 * nface), BF16)

    row16 = lax.broadcasted_iota(jnp.int32, (16, LANES), 0)
    col16 = lax.broadcasted_iota(jnp.int32, (16, LANES), 1)
    phase = [lax.rem(row16 - col16 + (p + 3 * LANES), 3) for p in range(3)]
    centred, ahead = [x == 0 for x in phase], [x == 1 for x in phase]
    band = [
        jnp.where(jnp.abs(row16 + 16 * r - col16) <= 1, 1.0, 0.0).astype(BF16) for r in range(LANES // 16)
    ]

    def matrix_tile(s, side, t, at):
        span = slice(t * LANES, (t + 1) * LANES)
        sums = [None] * (comp // 2)

        def add(q, part):
            sums[q] = part if sums[q] is None else sums[q] + part

        def row(d, a, b, rows):
            return jnp.broadcast_to(coef[d, a, b, side : side + 1, span], (rows, LANES))

        def inner(q, m):
            blocks = []
            for b in (2 * m, 2 * m + 1):
                line = []
                for a in (2 * q, 2 * q + 1):
                    mid, low, high = (row(d, a, b, 16).astype(BF16) for d in range(3))
                    mixed = [jnp.where(centred[p], mid, jnp.where(ahead[p], high, low)) for p in range(3)]
                    line.append(jnp.concatenate([mixed[r % 3] * band[r] for r in range(LANES // 16)], axis=0))
                blocks.append(jnp.concatenate(line, axis=1))
            pair = jnp.concatenate([z[s, b, :, pl.ds(at, LANES)] for b in (2 * m, 2 * m + 1)], axis=1)
            add(q, jnp.dot(pair, jnp.concatenate(blocks, axis=0), preferred_element_type=F32))

        def outer(qs):
            across = lax.broadcasted_iota(jnp.int32, (kdim, LANES), 1)
            edges = None
            for b in range(comp):
                ends = jnp.where(
                    across == LANES - 1, z[s, b, :, pl.ds(at - LANES, LANES)], z[s, b, :, pl.ds(at + LANES, LANES)]
                )
                ends = pltpu.roll(ends.astype(F32), 2 * b + 1, 1)
                edges = ends if edges is None else jnp.where(across < 2 * b, edges, ends)
            edges = edges.astype(BF16)
            for q in qs:
                line = []
                for a in (2 * q, 2 * q + 1):
                    grid = jnp.zeros((16, LANES), F32)
                    for b in range(comp):
                        grid = jnp.where((row16 == 2 * b) & (col16 == 0), row(1, a, b, 16), grid)
                        grid = jnp.where((row16 == 2 * b + 1) & (col16 == LANES - 1), row(2, a, b, 16), grid)
                    line.append(jnp.concatenate([grid, jnp.zeros((LANES - 16, LANES), F32)], axis=0).astype(BF16))
                add(q, jnp.dot(edges, jnp.concatenate(line, axis=1), preferred_element_type=F32))

        def finish(q):
            for e in range(2):
                applied[side, 2 * q + e, :, span] = sums[q][:, e * LANES : (e + 1) * LANES].astype(BF16)

        steps = [functools.partial(outer, range(comp // 2))]
        for q in range(comp // 2):
            steps += [functools.partial(inner, q, m) for m in range(comp // 2)]
            steps.append(functools.partial(finish, q))
        return steps

    def stencil(it, side, extra):
        i = it // chunks
        s = i * ny + side
        c0 = pl.multiple_of(lax.rem(it, chunks) * WIDE, WIDE)
        past = it if side else jnp.maximum(it - 1, 0)
        sp = past // chunks * ny + 1 - side
        cq = pl.multiple_of(lax.rem(past, chunks) * WIDE + LANES, LANES)
        total = []

        def tile_dot(a):
            total.append(
                lax.dot_general(
                    applied[1 - side, a], z[sp, a, :, pl.ds(cq, WIDE)], NT, preferred_element_type=F32
                )
            )

        tiles = all_tiles
        slots = {}
        if side == 0:
            tiles = all_tiles[: len(all_tiles) // 2]
            matrix = matrix_tile(s, side, 1, pl.multiple_of(c0 + 2 * LANES, LANES))
            for m, step in enumerate(matrix):
                slots.setdefault(m * len(tiles) // len(matrix), []).append(step)
        for a in range(comp):
            slots.setdefault(a * len(tiles) // comp, []).append(functools.partial(tile_dot, a))
        for m, step in enumerate(extra):
            slots.setdefault((2 * m + 1) * len(tiles) // (2 * len(extra)), []).append(step)

        for m, (t, k0) in enumerate(tiles):
            for step in slots.get(m, []):
                step()
            at = pl.multiple_of(c0 + (t + 1) * LANES, LANES)
            values = []
            for b in range(comp):
                here = z[s, b, k0 : k0 + ROWS, pl.ds(at, LANES)]
                low = jnp.where(last, z[s, b, k0 : k0 + ROWS, pl.ds(at - LANES, LANES)], here)
                high = jnp.where(first, z[s, b, k0 : k0 + ROWS, pl.ds(at + LANES, LANES)], here)
                values.append(
                    (
                        here.astype(F32),
                        pltpu.roll(low.astype(F32), 1, 1),
                        pltpu.roll(high.astype(F32), LANES - 1, 1),
                    )
                )
            for a in range(comp):
                acc = None
                for b in range(comp):
                    for d in range(3):
                        weight = coef[d, a, b, side : side + 1, t * LANES : (t + 1) * LANES]
                        term = weight * values[b][d]
                        acc = term if acc is None else acc + term
                applied[side, a, k0 : k0 + ROWS, t * LANES : (t + 1) * LANES] = acc.astype(BF16)
        diag_ref[sp] += functools.reduce(lambda p, q: p + q, total)

    def weights(it):
        i = it // chunks
        c0 = pl.multiple_of(lax.rem(it, chunks) * WIDE, WIDE)
        for d in range(3):
            for a in range(comp):
                coef[d, a] = jac[d, i, a, :, :, pl.ds(c0, WIDE)].astype(F32)

    def with_faces(it, carry):
        @pl.when((lax.rem(it, 2) == 1) & (it < 8 * nx - 1))
        def _():
            for copy in loads((it + 1) // 2):
                copy.wait()

        i = it // 8
        fs = i * ny + lax.rem(it, 2)
        block = lax.rem(it, 8) // 2

        def piece(h):
            pair, k = h % 2, h // 2
            k0 = pl.multiple_of(block * quarter + k * PIECE, PIECE)
            wanted = jnp.concatenate(
                [cells_ref[fs, 2 * pair : 2 * pair + 1], cells_ref[fs, 2 * pair + 1 : 2 * pair + 2]], axis=1
            )
            near = jnp.broadcast_to(wanted - k0, (16, 2 * nface)).astype(jnp.int16)
            pick = jnp.concatenate(
                [jnp.where(place == near - 16 * r, one, nil) for r in range(PIECE // 16)], axis=0
            )
            part = jnp.dot(
                z[fs, :, :, pl.ds(pl.multiple_of(k0 + LANES, LANES), PIECE)].reshape(comp * kdim, PIECE),
                pick,
                preferred_element_type=F32,
            )
            if k == 0:
                gather[fs, pair] = part + jnp.where(block == 0, 0.0, gather[fs, pair])
            else:
                gather[fs, pair] += part

        steps = [functools.partial(piece, h) for h in range(2 * quarter // PIECE)]
        weights(it)
        stencil(it, 0, steps[: len(steps) // 4])
        stencil(it, 1, steps[len(steps) // 4 :])
        return carry

    def without_faces(it, carry):
        weights(it)
        stencil(it, 0, [])
        stencil(it, 1, [])
        return carry

    for copy in loads(0):
        copy.wait()
    lax.fori_loop(0, 8 * nx, with_faces, 0)

    def push(s, carry):
        for d in range(4):
            picked = []
            for b in range(comp):
                values = gather[s, d // 2, b * kdim : (b + 1) * kdim, (d % 2) * nface : (d % 2 + 1) * nface]
                faces[s, d, :, b * nface : (b + 1) * nface] = values.astype(BF16)
                picked.append(values)
            for a in range(comp):
                acc = None
                for b in range(comp):
                    term = couple_ref[s, a, b].astype(F32)[d : d + 1] * picked[b]
                    acc = term if acc is None else acc + term
                pushed[s, d, :, a * nface : (a + 1) * nface] = acc.astype(BF16)
        return carry

    lax.fori_loop(0, subs, push, 0)

    pl.semaphore_wait(barrier, 4)

    def sources(d):
        if d == 0:
            return [(nx - 1) * ny + j for j in range(ny)]
        if d == 1:
            return list(range(ny))
        if d == 2:
            return [i * ny + ny - 1 for i in range(nx)]
        return [i * ny for i in range(nx)]

    sends = []
    for d in range(4):
        for m, s in enumerate(sources(d)):
            sends.append(
                pltpu.make_async_remote_copy(
                    src_ref=pushed.at[s, d],
                    dst_ref=arrived.at[d, m],
                    send_sem=send_sem.at[d, m],
                    recv_sem=recv_sem.at[d, m],
                    device_id=neighbour_of(d),
                    device_id_type=MESH,
                )
            )
    for copy in sends:
        copy.start()

    lax.fori_loop(8 * nx, nx * chunks, without_faces, 0)

    final = functools.reduce(
        lambda p, q: p + q,
        [
            lax.dot_general(
                applied[1, a], z[subs - 1, a, :, LANES + ncell - WIDE : LANES + ncell], NT,
                preferred_element_type=F32,
            )
            for a in range(comp)
        ],
    )
    diag_ref[subs - 1] += final
    for s in range(subs):
        diag_ref[s] = diag_ref[s].T

    def tile(s, e, right):
        return lax.dot_general(faces[s, e], right, NT, preferred_element_type=F32)

    steps_of = ((1, 0), (-1, 0), (0, 1), (0, -1))
    for i in range(nx):
        for j in range(ny):
            for e in range(4):
                ti, tj = i + steps_of[e][0], j + steps_of[e][1]
                if 0 <= ti < nx and 0 <= tj < ny:
                    off_ref[i * ny + j, e] = tile(i * ny + j, e, pushed[ti * ny + tj, OPPOSITE[e]])
    for copy in sends:
        copy.wait()
    for e in range(4):
        d = OPPOSITE[e]
        inside = has_neighbour(e)
        for m, s in enumerate(sources(e)):
            off_ref[s, e] = jnp.where(inside, tile(s, e, arrived[d, m]), 0.0)


def hand_over(diag_in, off_in, diag_out, off_out):
    diag_out[...] = diag_in[...]
    off_out[...] = off_in[...]


def on_device(z_basis, jac_center, jac_lower, jac_upper, face_cells, couple):
    nx, ny, comp, kdim, ncell = z_basis.shape
    nface = face_cells.shape[-1]
    subs = nx * ny
    merge = lambda array: array.reshape((subs,) + array.shape[2:])
    paired = [jnp.transpose(array, (0, 2, 3, 1, 4)) for array in (jac_center, jac_lower, jac_upper)]
    wide = comp * nface
    shapes = (
        jax.ShapeDtypeStruct((subs, kdim, kdim), F32),
        jax.ShapeDtypeStruct((subs, 4, kdim, kdim), F32),
    )
    results = pl.pallas_call(
        functools.partial(kernel, (nx, ny, comp, kdim, ncell, nface)),
        out_shape=shapes,
        in_specs=[pl.BlockSpec(memory_space=pl.ANY)] * 4 + [pl.BlockSpec(memory_space=pltpu.VMEM)] * 2,
        out_specs=[pl.BlockSpec(memory_space=pltpu.VMEM)] * 2,
        scratch_shapes=[
            pltpu.VMEM((subs, comp, kdim, ncell + 2 * LANES), BF16),
            pltpu.VMEM((3, nx, comp, comp, ny, ncell), BF16),
            pltpu.VMEM((3, comp, comp, ny, WIDE), F32),
            pltpu.VMEM((2, comp, kdim, WIDE), BF16),
            pltpu.VMEM((subs, 2, comp * kdim, 2 * nface), F32),
            pltpu.VMEM((subs, 4, kdim, wide), BF16),
            pltpu.VMEM((subs, 4, kdim, wide), BF16),
            pltpu.VMEM((4, 2, kdim, wide), BF16),
            pltpu.SemaphoreType.DMA((4 * nx, 3 + ny)),
            pltpu.SemaphoreType.DMA((4, 2)),
            pltpu.SemaphoreType.DMA((4, 2)),
        ],
        compiler_params=pltpu.CompilerParams(
            collective_id=0, has_side_effects=True, vmem_limit_bytes=56 * 2**20
        ),
        cost_estimate=pl.CostEstimate(flops=10**10, bytes_accessed=17 * 10**6, transcendentals=0),
    )(
        merge(z_basis), *paired, merge(face_cells), merge(jnp.transpose(couple, (0, 1, 3, 4, 2, 5)))
    )
    diag, off = pl.pallas_call(
        hand_over,
        out_shape=shapes,
        in_specs=[pl.BlockSpec(memory_space=pltpu.VMEM)] * 2,
        out_specs=[pl.BlockSpec(memory_space=pltpu.VMEM)] * 2,
    )(*results)
    return diag.reshape(nx, ny, kdim, kdim), off.reshape(nx, ny, 4, kdim, kdim)


def solution(mesh):
    in_specs = (
        P("sub", "col", None, None, None),
        P("sub", "col", None, None, None),
        P("sub", "col", None, None, None),
        P("sub", "col", None, None, None),
        P("sub", "col", None, None),
        P("sub", "col", None, None, None, None),
    )
    out_specs = (P("sub", "col", None, None), P("sub", "col", None, None, None))
    return jax.shard_map(
        on_device, mesh=mesh, in_specs=in_specs, out_specs=out_specs, check_vma=False
    )
```

```python
import functools

import jax
import jax.numpy as jnp
from jax import lax
from jax.experimental import pallas as pl
from jax.experimental.pallas import tpu as pltpu
from jax.sharding import PartitionSpec as P

MESH = pl.DeviceIdType.MESH
F32 = jnp.float32
BF16 = jnp.bfloat16
NT = (((1,), (1,)), ((), ()))
ROWS = 8
LANES = 128
WIDE = 256
PIECE = 512
OPPOSITE = (1, 0, 3, 2)


def neighbour_of(facing):
    sub, col = lax.axis_index("sub"), lax.axis_index("col")
    subs, cols = lax.axis_size("sub"), lax.axis_size("col")
    if facing == 0:
        return lax.rem(sub + 1, subs), col
    if facing == 1:
        return lax.rem(sub + subs - 1, subs), col
    if facing == 2:
        return sub, lax.rem(col + 1, cols)
    return sub, lax.rem(col + cols - 1, cols)


def has_neighbour(facing):
    sub, col = lax.axis_index("sub"), lax.axis_index("col")
    if facing == 0:
        return sub < lax.axis_size("sub") - 1
    if facing == 1:
        return sub > 0
    if facing == 2:
        return col < lax.axis_size("col") - 1
    return col > 0


def kernel(dims, z_hbm, jc_hbm, jl_hbm, ju_hbm, cells_hbm, couple_hbm, diag_ref, off_ref,
           z, jac, cells_ref, couple_ref, coef, applied, gather, faces, pushed, arrived, load_sem, small_sem, send_sem, recv_sem):
    nx, ny, comp, kdim, ncell, nface = dims
    subs = nx * ny
    chunks = ncell // WIDE
    quarter = ncell // 4
    all_tiles = [(t, k0) for t in range(WIDE // LANES) for k0 in range(0, kdim, ROWS)]

    def loads(n):
        i, at = n // 4, pl.multiple_of(lax.rem(n, 4) * quarter, quarter)
        pairs = [
            (z_hbm.at[i * ny + j, :, :, pl.ds(at, quarter)], z.at[i * ny + j, :, :, pl.ds(LANES + at, quarter)])
            for j in range(ny)
        ]
        pairs += [
            (ref.at[i, :, :, :, pl.ds(at, quarter)], jac.at[m, i, :, :, :, pl.ds(at, quarter)])
            for m, ref in enumerate((jc_hbm, jl_hbm, ju_hbm))
        ]
        return [pltpu.make_async_copy(src, dst, load_sem.at[n, m]) for m, (src, dst) in enumerate(pairs)]

    small = [
        pltpu.make_async_copy(src, dst, small_sem.at[n])
        for n, (src, dst) in enumerate(((cells_hbm, cells_ref), (couple_hbm, couple_ref)))
    ]
    small[0].start()
    for n in range(2):
        for copy in loads(n):
            copy.start()
    small[1].start()
    barrier = pltpu.get_barrier_semaphore()
    for facing in range(4):
        pl.semaphore_signal(barrier, inc=1, device_id=neighbour_of(facing), device_id_type=MESH)

    diag_ref[...] = jnp.zeros_like(diag_ref)
    applied[1] = jnp.zeros_like(applied[1])
    zero = jnp.zeros((comp, kdim, LANES), BF16)
    for s in range(subs):
        z[s, :, :, 0:LANES] = zero
        z[s, :, :, LANES + ncell :] = zero

    lane = lax.broadcasted_iota(jnp.int32, (ROWS, LANES), 1)
    first, last = lane == 0, lane == LANES - 1
    place = lax.broadcasted_iota(jnp.int32, (16, 2 * nface), 0).astype(jnp.int16)
    one, nil = jnp.ones((16, 2 * nface), BF16), jnp.zeros((16, 2 * nface), BF16)

    row16 = lax.broadcasted_iota(jnp.int32, (16, LANES), 0)
    col16 = lax.broadcasted_iota(jnp.int32, (16, LANES), 1)
    phase = [lax.rem(row16 - col16 + (p + 3 * LANES), 3) for p in range(3)]
    centred, ahead = [x == 0 for x in phase], [x == 1 for x in phase]
    band = [
        jnp.where(jnp.abs(row16 + 16 * r - col16) <= 1, 1.0, 0.0).astype(BF16) for r in range(LANES // 16)
    ]

    def matrix_tile(s, side, t, at):
        span = slice(t * LANES, (t + 1) * LANES)
        sums = [None] * (comp // 2)

        def add(q, part):
            sums[q] = part if sums[q] is None else sums[q] + part

        def row(d, a, b, rows):
            return jnp.broadcast_to(coef[d, a, b, side : side + 1, span], (rows, LANES))

        def inner(q, m):
            blocks = []
            for b in (2 * m, 2 * m + 1):
                line = []
                for a in (2 * q, 2 * q + 1):
                    mid, low, high = (row(d, a, b, 16).astype(BF16) for d in range(3))
                    mixed = [jnp.where(centred[p], mid, jnp.where(ahead[p], high, low)) for p in range(3)]
                    line.append(jnp.concatenate([mixed[r % 3] * band[r] for r in range(LANES // 16)], axis=0))
                blocks.append(jnp.concatenate(line, axis=1))
            pair = jnp.concatenate([z[s, b, :, pl.ds(at, LANES)] for b in (2 * m, 2 * m + 1)], axis=1)
            add(q, jnp.dot(pair, jnp.concatenate(blocks, axis=0), preferred_element_type=F32))

        def outer(qs):
            across = lax.broadcasted_iota(jnp.int32, (kdim, LANES), 1)
            edges = None
            for b in range(comp):
                ends = jnp.where(
                    across == LANES - 1, z[s, b, :, pl.ds(at - LANES, LANES)], z[s, b, :, pl.ds(at + LANES, LANES)]
                )
                ends = pltpu.roll(ends.astype(F32), 2 * b + 1, 1)
                edges = ends if edges is None else jnp.where(across < 2 * b, edges, ends)
            edges = edges.astype(BF16)[:, :16]
            for q in qs:
                line = []
                for a in (2 * q, 2 * q + 1):
                    grid = jnp.zeros((16, LANES), F32)
                    for b in range(comp):
                        grid = jnp.where((row16 == 2 * b) & (col16 == 0), row(1, a, b, 16), grid)
                        grid = jnp.where((row16 == 2 * b + 1) & (col16 == LANES - 1), row(2, a, b, 16), grid)
                    line.append(grid.astype(BF16))
                add(q, jnp.dot(edges, jnp.concatenate(line, axis=1), preferred_element_type=F32))

        def finish(q):
            for e in range(2):
                applied[side, 2 * q + e, :, span] = sums[q][:, e * LANES : (e + 1) * LANES].astype(BF16)

        steps = [functools.partial(outer, range(comp // 2))]
        for q in range(comp // 2):
            steps += [functools.partial(inner, q, m) for m in range(comp // 2)]
            steps.append(functools.partial(finish, q))
        return steps

    def stencil(it, side, extra, by_matrix):
        i = it // chunks
        s = i * ny + side
        c0 = pl.multiple_of(lax.rem(it, chunks) * WIDE, WIDE)
        past = it if side else jnp.maximum(it - 1, 0)
        sp = past // chunks * ny + 1 - side
        cq = pl.multiple_of(lax.rem(past, chunks) * WIDE + LANES, LANES)
        total = []

        def tile_dot(a):
            total.append(
                lax.dot_general(
                    applied[1 - side, a], z[sp, a, :, pl.ds(cq, WIDE)], NT, preferred_element_type=F32
                )
            )

        tiles = all_tiles
        slots = {}
        if by_matrix:
            tiles = all_tiles[: len(all_tiles) // 2]
            matrix = matrix_tile(s, side, 1, pl.multiple_of(c0 + 2 * LANES, LANES))
            for m, step in enumerate(matrix):
                slots.setdefault(m * len(tiles) // len(matrix), []).append(step)
        for a in range(comp):
            slots.setdefault(a * len(tiles) // comp, []).append(functools.partial(tile_dot, a))
        for m, step in enumerate(extra):
            slots.setdefault((2 * m + 1) * len(tiles) // (2 * len(extra)), []).append(step)

        for m, (t, k0) in enumerate(tiles):
            for step in slots.get(m, []):
                step()
            at = pl.multiple_of(c0 + (t + 1) * LANES, LANES)
            values = []
            for b in range(comp):
                here = z[s, b, k0 : k0 + ROWS, pl.ds(at, LANES)]
                low = jnp.where(last, z[s, b, k0 : k0 + ROWS, pl.ds(at - LANES, LANES)], here)
                high = jnp.where(first, z[s, b, k0 : k0 + ROWS, pl.ds(at + LANES, LANES)], here)
                values.append(
                    (
                        here.astype(F32),
                        pltpu.roll(low.astype(F32), 1, 1),
                        pltpu.roll(high.astype(F32), LANES - 1, 1),
                    )
                )
            for a in range(comp):
                acc = None
                for b in range(comp):
                    for d in range(3):
                        weight = coef[d, a, b, side : side + 1, t * LANES : (t + 1) * LANES]
                        term = weight * values[b][d]
                        acc = term if acc is None else acc + term
                applied[side, a, k0 : k0 + ROWS, t * LANES : (t + 1) * LANES] = acc.astype(BF16)
        diag_ref[sp] += functools.reduce(lambda p, q: p + q, total)

    def weights(it):
        i = it // chunks
        c0 = pl.multiple_of(lax.rem(it, chunks) * WIDE, WIDE)
        for d in range(3):
            for a in range(comp):
                coef[d, a] = jac[d, i, a, :, :, pl.ds(c0, WIDE)].astype(F32)

    def with_faces(it, carry):
        @pl.when((lax.rem(it, 2) == 1) & (it < 8 * nx - 1))
        def _():
            for copy in loads((it + 1) // 2):
                copy.wait()

        i = it // 8
        fs = i * ny + lax.rem(it, 2)
        block = lax.rem(it, 8) // 2

        def piece(h):
            pair, k = h % 2, h // 2
            k0 = pl.multiple_of(block * quarter + k * PIECE, PIECE)
            wanted = jnp.concatenate(
                [cells_ref[fs, 2 * pair : 2 * pair + 1], cells_ref[fs, 2 * pair + 1 : 2 * pair + 2]], axis=1
            )
            near = jnp.broadcast_to(wanted - k0, (16, 2 * nface)).astype(jnp.int16)
            pick = jnp.concatenate(
                [jnp.where(place == near - 16 * r, one, nil) for r in range(PIECE // 16)], axis=0
            )
            part = jnp.dot(
                z[fs, :, :, pl.ds(pl.multiple_of(k0 + LANES, LANES), PIECE)].reshape(comp * kdim, PIECE),
                pick,
                preferred_element_type=F32,
            )
            if k == 0:
                gather[fs, pair] = part + jnp.where(block == 0, 0.0, gather[fs, pair])
            else:
                gather[fs, pair] += part

        steps = [functools.partial(piece, h) for h in range(2 * quarter // PIECE)]
        weights(it)
        stencil(it, 0, steps[:1], True)
        stencil(it, 1, steps[1:], False)
        return carry

    def without_faces(it, carry):
        weights(it)
        stencil(it, 0, [], True)
        stencil(it, 1, [], True)
        return carry

    small[0].wait()
    for copy in loads(0):
        copy.wait()
    for n in range(2, 4 * nx):
        for copy in loads(n):
            copy.start()
    lax.fori_loop(0, 8 * nx, with_faces, 0)

    def push(s, carry):
        for d in range(4):
            picked = []
            for b in range(comp):
                values = gather[s, d // 2, b * kdim : (b + 1) * kdim, (d % 2) * nface : (d % 2 + 1) * nface]
                faces[s, d, :, b * nface : (b + 1) * nface] = values.astype(BF16)
                picked.append(values)
            for a in range(comp):
                acc = None
                for b in range(comp):
                    term = couple_ref[s, a, b].astype(F32)[d : d + 1] * picked[b]
                    acc = term if acc is None else acc + term
                pushed[s, d, :, a * nface : (a + 1) * nface] = acc.astype(BF16)
        return carry

    small[1].wait()
    lax.fori_loop(0, subs, push, 0)

    pl.semaphore_wait(barrier, 4)

    def sources(d):
        if d == 0:
            return [(nx - 1) * ny + j for j in range(ny)]
        if d == 1:
            return list(range(ny))
        if d == 2:
            return [i * ny + ny - 1 for i in range(nx)]
        return [i * ny for i in range(nx)]

    sends = []
    for d in range(4):
        for m, s in enumerate(sources(d)):
            sends.append(
                pltpu.make_async_remote_copy(
                    src_ref=pushed.at[s, d],
                    dst_ref=arrived.at[d, m],
                    send_sem=send_sem.at[d, m],
                    recv_sem=recv_sem.at[d, m],
                    device_id=neighbour_of(d),
                    device_id_type=MESH,
                )
            )
    for copy in sends:
        copy.start()

    lax.fori_loop(8 * nx, nx * chunks, without_faces, 0)

    final = functools.reduce(
        lambda p, q: p + q,
        [
            lax.dot_general(
                applied[1, a], z[subs - 1, a, :, LANES + ncell - WIDE : LANES + ncell], NT,
                preferred_element_type=F32,
            )
            for a in range(comp)
        ],
    )
    diag_ref[subs - 1] += final
    for s in range(subs):
        diag_ref[s] = diag_ref[s].T

    def tile(s, e, right):
        return lax.dot_general(faces[s, e], right, NT, preferred_element_type=F32)

    steps_of = ((1, 0), (-1, 0), (0, 1), (0, -1))
    for i in range(nx):
        for j in range(ny):
            for e in range(4):
                ti, tj = i + steps_of[e][0], j + steps_of[e][1]
                if 0 <= ti < nx and 0 <= tj < ny:
                    off_ref[i * ny + j, e] = tile(i * ny + j, e, pushed[ti * ny + tj, OPPOSITE[e]])
    for copy in sends:
        copy.wait()
    for e in range(4):
        d = OPPOSITE[e]
        inside = has_neighbour(e)
        for m, s in enumerate(sources(e)):
            off_ref[s, e] = jnp.where(inside, tile(s, e, arrived[d, m]), 0.0)


def hand_over(diag_in, off_in, diag_out, off_out, diag, off, sems):
    parts = [(diag_in, diag, diag_out)]
    parts += [(off_in.at[s], off.at[s], off_out.at[s]) for s in range(off_in.shape[0])]
    reads = [pltpu.make_async_copy(a, b, sems.at[0, n]) for n, (a, b, _) in enumerate(parts)]
    writes = [pltpu.make_async_copy(b, c, sems.at[1, n]) for n, (_, b, c) in enumerate(parts)]
    for copy in reads:
        copy.start()
    for read, write in zip(reads, writes):
        read.wait()
        write.start()
    for copy in writes:
        copy.wait()


def on_device(z_basis, jac_center, jac_lower, jac_upper, face_cells, couple):
    nx, ny, comp, kdim, ncell = z_basis.shape
    nface = face_cells.shape[-1]
    subs = nx * ny
    merge = lambda array: array.reshape((subs,) + array.shape[2:])
    paired = [jnp.transpose(array, (0, 2, 3, 1, 4)) for array in (jac_center, jac_lower, jac_upper)]
    wide = comp * nface
    shapes = (
        jax.ShapeDtypeStruct((subs, kdim, kdim), F32),
        jax.ShapeDtypeStruct((subs, 4, kdim, kdim), F32),
    )
    results = pl.pallas_call(
        functools.partial(kernel, (nx, ny, comp, kdim, ncell, nface)),
        out_shape=shapes,
        in_specs=[pl.BlockSpec(memory_space=pl.ANY)] * 6,
        out_specs=[pl.BlockSpec(memory_space=pltpu.VMEM)] * 2,
        scratch_shapes=[
            pltpu.VMEM((subs, comp, kdim, ncell + 2 * LANES), BF16),
            pltpu.VMEM((3, nx, comp, comp, ny, ncell), BF16),
            pltpu.VMEM((subs, 4, nface), jnp.int32),
            pltpu.VMEM((subs, comp, comp, 4, nface), BF16),
            pltpu.VMEM((3, comp, comp, ny, WIDE), F32),
            pltpu.VMEM((2, comp, kdim, WIDE), BF16),
            pltpu.VMEM((subs, 2, comp * kdim, 2 * nface), F32),
            pltpu.VMEM((subs, 4, kdim, wide), BF16),
            pltpu.VMEM((subs, 4, kdim, wide), BF16),
            pltpu.VMEM((4, 2, kdim, wide), BF16),
            pltpu.SemaphoreType.DMA((4 * nx, 3 + ny)),
            pltpu.SemaphoreType.DMA((2,)),
            pltpu.SemaphoreType.DMA((4, 2)),
            pltpu.SemaphoreType.DMA((4, 2)),
        ],
        compiler_params=pltpu.CompilerParams(
            collective_id=0, has_side_effects=True, vmem_limit_bytes=56 * 2**20
        ),
        cost_estimate=pl.CostEstimate(flops=10**10, bytes_accessed=17 * 10**6, transcendentals=0),
    )(
        merge(z_basis), *paired, merge(face_cells), merge(jnp.transpose(couple, (0, 1, 3, 4, 2, 5)))
    )
    diag, off = pl.pallas_call(
        hand_over,
        out_shape=shapes,
        in_specs=[pl.BlockSpec(memory_space=pl.ANY)] * 2,
        out_specs=[pl.BlockSpec(memory_space=pl.ANY)] * 2,
        scratch_shapes=[
            pltpu.VMEM(shapes[0].shape, F32),
            pltpu.VMEM(shapes[1].shape, F32),
            pltpu.SemaphoreType.DMA((2, 1 + subs)),
        ],
        compiler_params=pltpu.CompilerParams(vmem_limit_bytes=56 * 2**20),
    )(*results)
    return diag.reshape(nx, ny, kdim, kdim), off.reshape(nx, ny, 4, kdim, kdim)


def solution(mesh):
    in_specs = (
        P("sub", "col", None, None, None),
        P("sub", "col", None, None, None),
        P("sub", "col", None, None, None),
        P("sub", "col", None, None, None),
        P("sub", "col", None, None),
        P("sub", "col", None, None, None, None),
    )
    out_specs = (P("sub", "col", None, None), P("sub", "col", None, None, None))
    return jax.shard_map(
        on_device, mesh=mesh, in_specs=in_specs, out_specs=out_specs, check_vma=False
    )
```

```python
import functools

import jax
import jax.numpy as jnp
from jax import lax
from jax.experimental import pallas as pl
from jax.experimental.pallas import tpu as pltpu
from jax.sharding import PartitionSpec as P

MESH = pl.DeviceIdType.MESH
F32 = jnp.float32
BF16 = jnp.bfloat16
NT = (((1,), (1,)), ((), ()))
ROWS = 8
LANES = 128
WIDE = 256
PIECE = 512
OPPOSITE = (1, 0, 3, 2)


def neighbour_of(facing):
    sub, col = lax.axis_index("sub"), lax.axis_index("col")
    subs, cols = lax.axis_size("sub"), lax.axis_size("col")
    if facing == 0:
        return lax.rem(sub + 1, subs), col
    if facing == 1:
        return lax.rem(sub + subs - 1, subs), col
    if facing == 2:
        return sub, lax.rem(col + 1, cols)
    return sub, lax.rem(col + cols - 1, cols)


def has_neighbour(facing):
    sub, col = lax.axis_index("sub"), lax.axis_index("col")
    if facing == 0:
        return sub < lax.axis_size("sub") - 1
    if facing == 1:
        return sub > 0
    if facing == 2:
        return col < lax.axis_size("col") - 1
    return col > 0


def kernel(dims, z_hbm, jc_hbm, jl_hbm, ju_hbm, cells_hbm, couple_hbm, diag_ref, off_ref,
           z, jac, cells_ref, couple_ref, coef, applied, gather, faces, pushed, arrived, load_sem, small_sem, send_sem, recv_sem):
    nx, ny, comp, kdim, ncell, nface = dims
    subs = nx * ny
    chunks = ncell // WIDE
    quarter = ncell // 4
    all_tiles = [(t, k0) for t in range(WIDE // LANES) for k0 in range(0, kdim, ROWS)]

    def loads(n):
        i, at = n // 4, pl.multiple_of(lax.rem(n, 4) * quarter, quarter)
        pairs = [
            (z_hbm.at[i * ny + j, :, :, pl.ds(at, quarter)], z.at[i * ny + j, :, :, pl.ds(LANES + at, quarter)])
            for j in range(ny)
        ]
        pairs += [
            (ref.at[i, :, :, :, pl.ds(at, quarter)], jac.at[m, i, :, :, :, pl.ds(at, quarter)])
            for m, ref in enumerate((jc_hbm, jl_hbm, ju_hbm))
        ]
        return [pltpu.make_async_copy(src, dst, load_sem.at[n, m]) for m, (src, dst) in enumerate(pairs)]

    small = [
        pltpu.make_async_copy(src, dst, small_sem.at[n])
        for n, (src, dst) in enumerate(((cells_hbm, cells_ref), (couple_hbm, couple_ref)))
    ]
    small[0].start()
    for n in range(2):
        for copy in loads(n):
            copy.start()
    small[1].start()
    barrier = pltpu.get_barrier_semaphore()
    for facing in range(4):
        pl.semaphore_signal(barrier, inc=1, device_id=neighbour_of(facing), device_id_type=MESH)

    diag_ref[...] = jnp.zeros_like(diag_ref)
    applied[1] = jnp.zeros_like(applied[1])
    zero = jnp.zeros((comp, kdim, LANES), BF16)
    for s in range(subs):
        z[s, :, :, 0:LANES] = zero
        z[s, :, :, LANES + ncell :] = zero

    lane = lax.broadcasted_iota(jnp.int32, (ROWS, LANES), 1)
    first, last = lane == 0, lane == LANES - 1
    place = lax.broadcasted_iota(jnp.int32, (16, 2 * nface), 0).astype(jnp.int16)
    one, nil = jnp.ones((16, 2 * nface), BF16), jnp.zeros((16, 2 * nface), BF16)

    row16 = lax.broadcasted_iota(jnp.int32, (16, LANES), 0)
    col16 = lax.broadcasted_iota(jnp.int32, (16, LANES), 1)
    phase = [lax.rem(row16 - col16 + (p + 3 * LANES), 3) for p in range(3)]
    centred, ahead = [x == 0 for x in phase], [x == 1 for x in phase]
    band = [
        jnp.where(jnp.abs(row16 + 16 * r - col16) <= 1, 1.0, 0.0).astype(BF16) for r in range(LANES // 16)
    ]

    def matrix_tile(s, side, t, at):
        span = slice(t * LANES, (t + 1) * LANES)
        sums = [None] * (comp // 2)

        def add(q, part):
            sums[q] = part if sums[q] is None else sums[q] + part

        def row(d, a, b, rows):
            return jnp.broadcast_to(coef[d, a, b, side : side + 1, span], (rows, LANES))

        def inner(q, m):
            blocks = []
            for b in (2 * m, 2 * m + 1):
                line = []
                for a in (2 * q, 2 * q + 1):
                    mid, low, high = (row(d, a, b, 16).astype(BF16) for d in range(3))
                    mixed = [jnp.where(centred[p], mid, jnp.where(ahead[p], high, low)) for p in range(3)]
                    line.append(jnp.concatenate([mixed[r % 3] * band[r] for r in range(LANES // 16)], axis=0))
                blocks.append(jnp.concatenate(line, axis=1))
            pair = jnp.concatenate([z[s, b, :, pl.ds(at, LANES)] for b in (2 * m, 2 * m + 1)], axis=1)
            add(q, jnp.dot(pair, jnp.concatenate(blocks, axis=0), preferred_element_type=F32))

        def outer(qs):
            across = lax.broadcasted_iota(jnp.int32, (kdim, LANES), 1)
            edges = None
            for b in range(comp):
                ends = jnp.where(
                    across == LANES - 1, z[s, b, :, pl.ds(at - LANES, LANES)], z[s, b, :, pl.ds(at + LANES, LANES)]
                )
                ends = pltpu.roll(ends.astype(F32), 2 * b + 1, 1)
                edges = ends if edges is None else jnp.where(across < 2 * b, edges, ends)
            edges = edges.astype(BF16)[:, :16]
            for q in qs:
                line = []
                for a in (2 * q, 2 * q + 1):
                    grid = jnp.zeros((16, LANES), F32)
                    for b in range(comp):
                        grid = jnp.where((row16 == 2 * b) & (col16 == 0), row(1, a, b, 16), grid)
                        grid = jnp.where((row16 == 2 * b + 1) & (col16 == LANES - 1), row(2, a, b, 16), grid)
                    line.append(grid.astype(BF16))
                add(q, jnp.dot(edges, jnp.concatenate(line, axis=1), preferred_element_type=F32))

        def finish(q):
            for e in range(2):
                applied[side, 2 * q + e, :, span] = sums[q][:, e * LANES : (e + 1) * LANES].astype(BF16)

        steps = [functools.partial(outer, range(comp // 2))]
        for q in range(comp // 2):
            steps += [functools.partial(inner, q, m) for m in range(comp // 2)]
            steps.append(functools.partial(finish, q))
        return steps

    def stencil(it, side, extra, by_matrix):
        i = it // chunks
        s = i * ny + side
        c0 = pl.multiple_of(lax.rem(it, chunks) * WIDE, WIDE)
        past = it if side else jnp.maximum(it - 1, 0)
        sp = past // chunks * ny + 1 - side
        cq = pl.multiple_of(lax.rem(past, chunks) * WIDE + LANES, LANES)
        total = []

        def tile_dot(a):
            total.append(
                lax.dot_general(
                    applied[1 - side, a], z[sp, a, :, pl.ds(cq, WIDE)], NT, preferred_element_type=F32
                )
            )

        tiles = all_tiles
        slots = {}
        if by_matrix:
            tiles = all_tiles[: len(all_tiles) // 2]
            matrix = matrix_tile(s, side, 1, pl.multiple_of(c0 + 2 * LANES, LANES))
            for m, step in enumerate(matrix):
                slots.setdefault(m * len(tiles) // len(matrix), []).append(step)
        for a in range(comp):
            slots.setdefault(a * len(tiles) // comp, []).append(functools.partial(tile_dot, a))
        for m, step in enumerate(extra):
            slots.setdefault(m * len(tiles) // len(extra), []).append(step)

        for m, (t, k0) in enumerate(tiles):
            for step in slots.get(m, []):
                step()
            at = pl.multiple_of(c0 + (t + 1) * LANES, LANES)
            values = []
            for b in range(comp):
                here = z[s, b, k0 : k0 + ROWS, pl.ds(at, LANES)]
                low = jnp.where(last, z[s, b, k0 : k0 + ROWS, pl.ds(at - LANES, LANES)], here)
                high = jnp.where(first, z[s, b, k0 : k0 + ROWS, pl.ds(at + LANES, LANES)], here)
                values.append(
                    (
                        here.astype(F32),
                        pltpu.roll(low.astype(F32), 1, 1),
                        pltpu.roll(high.astype(F32), LANES - 1, 1),
                    )
                )
            for a in range(comp):
                acc = None
                for b in range(comp):
                    for d in range(3):
                        weight = coef[d, a, b, side : side + 1, t * LANES : (t + 1) * LANES]
                        term = weight * values[b][d]
                        acc = term if acc is None else acc + term
                applied[side, a, k0 : k0 + ROWS, t * LANES : (t + 1) * LANES] = acc.astype(BF16)
        diag_ref[sp] += functools.reduce(lambda p, q: p + q, total)

    def weights(it):
        i = it // chunks
        c0 = pl.multiple_of(lax.rem(it, chunks) * WIDE, WIDE)
        for d in range(3):
            for a in range(comp):
                coef[d, a] = jac[d, i, a, :, :, pl.ds(c0, WIDE)].astype(F32)

    def with_faces(it, carry):
        @pl.when((lax.rem(it, 2) == 1) & (it < 8 * nx - 1))
        def _():
            for copy in loads((it + 1) // 2):
                copy.wait()

        i = it // 8
        fs = i * ny + lax.rem(it, 2)
        block = lax.rem(it, 8) // 2

        def piece(h):
            pair, k = h % 2, h // 2
            k0 = pl.multiple_of(block * quarter + k * PIECE, PIECE)
            wanted = jnp.concatenate(
                [cells_ref[fs, 2 * pair : 2 * pair + 1], cells_ref[fs, 2 * pair + 1 : 2 * pair + 2]], axis=1
            )
            near = jnp.broadcast_to(wanted - k0, (16, 2 * nface)).astype(jnp.int16)
            pick = jnp.concatenate(
                [jnp.where(place == near - 16 * r, one, nil) for r in range(PIECE // 16)], axis=0
            )
            part = jnp.dot(
                z[fs, :, :, pl.ds(pl.multiple_of(k0 + LANES, LANES), PIECE)].reshape(comp * kdim, PIECE),
                pick,
                preferred_element_type=F32,
            )
            if k == 0:
                gather[fs, pair] = part + jnp.where(block == 0, 0.0, gather[fs, pair])
            else:
                gather[fs, pair] += part

        steps = [functools.partial(piece, h) for h in range(2 * quarter // PIECE)]
        weights(it)
        stencil(it, 0, steps[:1], True)
        stencil(it, 1, steps[1:], False)
        return carry

    def without_faces(it, carry):
        weights(it)
        stencil(it, 0, [], True)
        stencil(it, 1, [], True)
        return carry

    small[0].wait()
    for copy in loads(0):
        copy.wait()
    for n in range(2, 4 * nx):
        for copy in loads(n):
            copy.start()
    lax.fori_loop(0, 8 * nx, with_faces, 0)

    def push(s, carry):
        for d in range(4):
            picked = []
            for b in range(comp):
                values = gather[s, d // 2, b * kdim : (b + 1) * kdim, (d % 2) * nface : (d % 2 + 1) * nface]
                faces[s, d, :, b * nface : (b + 1) * nface] = values.astype(BF16)
                picked.append(values)
            for a in range(comp):
                acc = None
                for b in range(comp):
                    term = couple_ref[s, a, b].astype(F32)[d : d + 1] * picked[b]
                    acc = term if acc is None else acc + term
                pushed[s, d, :, a * nface : (a + 1) * nface] = acc.astype(BF16)
        return carry

    small[1].wait()
    def tile(s, e, right):
        return lax.dot_general(faces[s, e], right, NT, preferred_element_type=F32)

    steps_of = ((1, 0), (-1, 0), (0, 1), (0, -1))
    for s in range(subs):
        push(s, 0)
        for e in range(4):
            ti, tj = s // ny + steps_of[e][0], s % ny + steps_of[e][1]
            other = ti * ny + tj
            if 0 <= ti < nx and 0 <= tj < ny and other < s:
                off_ref[s, e] = tile(s, e, pushed[other, OPPOSITE[e]])
                off_ref[other, OPPOSITE[e]] = tile(other, OPPOSITE[e], pushed[s, e])

    pl.semaphore_wait(barrier, 4)

    def sources(d):
        if d == 0:
            return [(nx - 1) * ny + j for j in range(ny)]
        if d == 1:
            return list(range(ny))
        if d == 2:
            return [i * ny + ny - 1 for i in range(nx)]
        return [i * ny for i in range(nx)]

    sends = []
    for d in range(4):
        for m, s in enumerate(sources(d)):
            sends.append(
                pltpu.make_async_remote_copy(
                    src_ref=pushed.at[s, d],
                    dst_ref=arrived.at[d, m],
                    send_sem=send_sem.at[d, m],
                    recv_sem=recv_sem.at[d, m],
                    device_id=neighbour_of(d),
                    device_id_type=MESH,
                )
            )
    for copy in sends:
        copy.start()

    lax.fori_loop(8 * nx, nx * chunks, without_faces, 0)

    final = functools.reduce(
        lambda p, q: p + q,
        [
            lax.dot_general(
                applied[1, a], z[subs - 1, a, :, LANES + ncell - WIDE : LANES + ncell], NT,
                preferred_element_type=F32,
            )
            for a in range(comp)
        ],
    )
    diag_ref[subs - 1] += final
    for s in range(subs):
        diag_ref[s] = diag_ref[s].T

    for copy in sends:
        copy.wait()
    for e in range(4):
        d = OPPOSITE[e]
        inside = has_neighbour(e)
        for m, s in enumerate(sources(e)):
            off_ref[s, e] = jnp.where(inside, tile(s, e, arrived[d, m]), 0.0)


def hand_over(diag_in, off_in, diag_out, off_out, diag, off, sems):
    parts = [(diag_in, diag, diag_out)]
    parts += [(off_in.at[s], off.at[s], off_out.at[s]) for s in range(off_in.shape[0])]
    reads = [pltpu.make_async_copy(a, b, sems.at[0, n]) for n, (a, b, _) in enumerate(parts)]
    writes = [pltpu.make_async_copy(b, c, sems.at[1, n]) for n, (_, b, c) in enumerate(parts)]
    for copy in reads:
        copy.start()
    for read, write in zip(reads, writes):
        read.wait()
        write.start()
    for copy in writes:
        copy.wait()


def on_device(z_basis, jac_center, jac_lower, jac_upper, face_cells, couple):
    nx, ny, comp, kdim, ncell = z_basis.shape
    nface = face_cells.shape[-1]
    subs = nx * ny
    merge = lambda array: array.reshape((subs,) + array.shape[2:])
    paired = [jnp.transpose(array, (0, 2, 3, 1, 4)) for array in (jac_center, jac_lower, jac_upper)]
    wide = comp * nface
    shapes = (
        jax.ShapeDtypeStruct((subs, kdim, kdim), F32),
        jax.ShapeDtypeStruct((subs, 4, kdim, kdim), F32),
    )
    results = pl.pallas_call(
        functools.partial(kernel, (nx, ny, comp, kdim, ncell, nface)),
        out_shape=shapes,
        in_specs=[pl.BlockSpec(memory_space=pl.ANY)] * 6,
        out_specs=[pl.BlockSpec(memory_space=pltpu.VMEM)] * 2,
        scratch_shapes=[
            pltpu.VMEM((subs, comp, kdim, ncell + 2 * LANES), BF16),
            pltpu.VMEM((3, nx, comp, comp, ny, ncell), BF16),
            pltpu.VMEM((subs, 4, nface), jnp.int32),
            pltpu.VMEM((subs, comp, comp, 4, nface), BF16),
            pltpu.VMEM((3, comp, comp, ny, WIDE), F32),
            pltpu.VMEM((2, comp, kdim, WIDE), BF16),
            pltpu.VMEM((subs, 2, comp * kdim, 2 * nface), F32),
            pltpu.VMEM((subs, 4, kdim, wide), BF16),
            pltpu.VMEM((subs, 4, kdim, wide), BF16),
            pltpu.VMEM((4, 2, kdim, wide), BF16),
            pltpu.SemaphoreType.DMA((4 * nx, 3 + ny)),
            pltpu.SemaphoreType.DMA((2,)),
            pltpu.SemaphoreType.DMA((4, 2)),
            pltpu.SemaphoreType.DMA((4, 2)),
        ],
        compiler_params=pltpu.CompilerParams(
            collective_id=0, has_side_effects=True, vmem_limit_bytes=56 * 2**20
        ),
        cost_estimate=pl.CostEstimate(flops=10**10, bytes_accessed=17 * 10**6, transcendentals=0),
    )(
        merge(z_basis), *paired, merge(face_cells), merge(jnp.transpose(couple, (0, 1, 3, 4, 2, 5)))
    )
    diag, off = pl.pallas_call(
        hand_over,
        out_shape=shapes,
        in_specs=[pl.BlockSpec(memory_space=pl.ANY)] * 2,
        out_specs=[pl.BlockSpec(memory_space=pl.ANY)] * 2,
        scratch_shapes=[
            pltpu.VMEM(shapes[0].shape, F32),
            pltpu.VMEM(shapes[1].shape, F32),
            pltpu.SemaphoreType.DMA((2, 1 + subs)),
        ],
        compiler_params=pltpu.CompilerParams(vmem_limit_bytes=56 * 2**20),
    )(*results)
    return diag.reshape(nx, ny, kdim, kdim), off.reshape(nx, ny, 4, kdim, kdim)


def solution(mesh):
    in_specs = (
        P("sub", "col", None, None, None),
        P("sub", "col", None, None, None),
        P("sub", "col", None, None, None),
        P("sub", "col", None, None, None),
        P("sub", "col", None, None),
        P("sub", "col", None, None, None, None),
    )
    out_specs = (P("sub", "col", None, None), P("sub", "col", None, None, None))
    return jax.shard_map(
        on_device, mesh=mesh, in_specs=in_specs, out_specs=out_specs, check_vma=False
    )
```

```python
import functools

import jax
import jax.numpy as jnp
from jax import lax
from jax.experimental import pallas as pl
from jax.experimental.pallas import tpu as pltpu
from jax.sharding import PartitionSpec as P

MESH = pl.DeviceIdType.MESH
F32 = jnp.float32
BF16 = jnp.bfloat16
NT = (((1,), (1,)), ((), ()))
ROWS = 8
LANES = 128
WIDE = 256
PIECE = 512
OPPOSITE = (1, 0, 3, 2)


def neighbour_of(facing):
    sub, col = lax.axis_index("sub"), lax.axis_index("col")
    subs, cols = lax.axis_size("sub"), lax.axis_size("col")
    if facing == 0:
        return lax.rem(sub + 1, subs), col
    if facing == 1:
        return lax.rem(sub + subs - 1, subs), col
    if facing == 2:
        return sub, lax.rem(col + 1, cols)
    return sub, lax.rem(col + cols - 1, cols)


def has_neighbour(facing):
    sub, col = lax.axis_index("sub"), lax.axis_index("col")
    if facing == 0:
        return sub < lax.axis_size("sub") - 1
    if facing == 1:
        return sub > 0
    if facing == 2:
        return col < lax.axis_size("col") - 1
    return col > 0


def kernel(dims, z_hbm, jc_hbm, jl_hbm, ju_hbm, cells_hbm, couple_hbm, diag_ref, off_ref,
           z, jac, cells_ref, couple_ref, coef, applied, gather, faces, pushed, arrived, load_sem, small_sem, send_sem, recv_sem):
    nx, ny, comp, kdim, ncell, nface = dims
    subs = nx * ny
    chunks = ncell // WIDE
    quarter = ncell // 4
    all_tiles = [(t, k0) for t in range(WIDE // LANES) for k0 in range(0, kdim, ROWS)]

    def loads(n):
        i, at = n // 4, pl.multiple_of(lax.rem(n, 4) * quarter, quarter)
        pairs = [
            (z_hbm.at[i * ny + j, :, :, pl.ds(at, quarter)], z.at[i * ny + j, :, :, pl.ds(LANES + at, quarter)])
            for j in range(ny)
        ]
        pairs += [
            (ref.at[i, :, :, :, pl.ds(at, quarter)], jac.at[m, i, :, :, :, pl.ds(at, quarter)])
            for m, ref in enumerate((jc_hbm, jl_hbm, ju_hbm))
        ]
        return [pltpu.make_async_copy(src, dst, load_sem.at[n, m]) for m, (src, dst) in enumerate(pairs)]

    small = [
        pltpu.make_async_copy(src, dst, small_sem.at[n])
        for n, (src, dst) in enumerate(((cells_hbm, cells_ref), (couple_hbm, couple_ref)))
    ]
    small[0].start()
    for n in range(2):
        for copy in loads(n):
            copy.start()
    small[1].start()
    barrier = pltpu.get_barrier_semaphore()
    for facing in range(4):
        pl.semaphore_signal(barrier, inc=1, device_id=neighbour_of(facing), device_id_type=MESH)

    diag_ref[...] = jnp.zeros_like(diag_ref)
    applied[1] = jnp.zeros_like(applied[1])
    zero = jnp.zeros((comp, kdim, LANES), BF16)
    for s in range(subs):
        z[s, :, :, 0:LANES] = zero
        z[s, :, :, LANES + ncell :] = zero

    lane = lax.broadcasted_iota(jnp.int32, (ROWS, LANES), 1)
    first, last = lane == 0, lane == LANES - 1
    place = lax.broadcasted_iota(jnp.int32, (16, 2 * nface), 0).astype(jnp.int16)
    one, nil = jnp.ones((16, 2 * nface), BF16), jnp.zeros((16, 2 * nface), BF16)

    row16 = lax.broadcasted_iota(jnp.int32, (16, LANES), 0)
    col16 = lax.broadcasted_iota(jnp.int32, (16, LANES), 1)
    phase = [lax.rem(row16 - col16 + (p + 3 * LANES), 3) for p in range(3)]
    centred, ahead = [x == 0 for x in phase], [x == 1 for x in phase]
    band = [
        jnp.where(jnp.abs(row16 + 16 * r - col16) <= 1, 1.0, 0.0).astype(BF16) for r in range(LANES // 16)
    ]

    def matrix_tile(s, side, t, at):
        span = slice(t * LANES, (t + 1) * LANES)
        sums = [None] * (comp // 2)

        def add(q, part):
            sums[q] = part if sums[q] is None else sums[q] + part

        def row(d, a, b, rows):
            return jnp.broadcast_to(coef[d, a, b, side : side + 1, span], (rows, LANES))

        def inner(q, m):
            blocks = []
            for b in (2 * m, 2 * m + 1):
                line = []
                for a in (2 * q, 2 * q + 1):
                    mid, low, high = (row(d, a, b, 16).astype(BF16) for d in range(3))
                    mixed = [jnp.where(centred[p], mid, jnp.where(ahead[p], high, low)) for p in range(3)]
                    line.append(jnp.concatenate([mixed[r % 3] * band[r] for r in range(LANES // 16)], axis=0))
                blocks.append(jnp.concatenate(line, axis=1))
            pair = jnp.concatenate([z[s, b, :, pl.ds(at, LANES)] for b in (2 * m, 2 * m + 1)], axis=1)
            add(q, jnp.dot(pair, jnp.concatenate(blocks, axis=0), preferred_element_type=F32))

        def outer(qs):
            across = lax.broadcasted_iota(jnp.int32, (kdim, LANES), 1)
            edges = None
            for b in range(comp):
                ends = jnp.where(
                    across == LANES - 1, z[s, b, :, pl.ds(at - LANES, LANES)], z[s, b, :, pl.ds(at + LANES, LANES)]
                )
                ends = pltpu.roll(ends.astype(F32), 2 * b + 1, 1)
                edges = ends if edges is None else jnp.where(across < 2 * b, edges, ends)
            edges = edges.astype(BF16)[:, :16]
            for q in qs:
                line = []
                for a in (2 * q, 2 * q + 1):
                    grid = jnp.zeros((16, LANES), F32)
                    for b in range(comp):
                        grid = jnp.where((row16 == 2 * b) & (col16 == 0), row(1, a, b, 16), grid)
                        grid = jnp.where((row16 == 2 * b + 1) & (col16 == LANES - 1), row(2, a, b, 16), grid)
                    line.append(grid.astype(BF16))
                add(q, jnp.dot(edges, jnp.concatenate(line, axis=1), preferred_element_type=F32))

        def finish(q):
            for e in range(2):
                applied[side, 2 * q + e, :, span] = sums[q][:, e * LANES : (e + 1) * LANES].astype(BF16)

        steps = [functools.partial(outer, range(comp // 2))]
        for q in range(comp // 2):
            steps += [functools.partial(inner, q, m) for m in range(comp // 2)]
            steps.append(functools.partial(finish, q))
        return steps

    def stencil(it, side, extra, by_matrix):
        i = it // chunks
        s = i * ny + side
        c0 = pl.multiple_of(lax.rem(it, chunks) * WIDE, WIDE)
        past = it if side else jnp.maximum(it - 1, 0)
        sp = past // chunks * ny + 1 - side
        cq = pl.multiple_of(lax.rem(past, chunks) * WIDE + LANES, LANES)
        total = []

        def tile_dot(a):
            total.append(
                lax.dot_general(
                    applied[1 - side, a], z[sp, a, :, pl.ds(cq, WIDE)], NT, preferred_element_type=F32
                )
            )

        tiles = all_tiles
        slots = {}
        if by_matrix:
            tiles = all_tiles[: len(all_tiles) // 2]
            matrix = matrix_tile(s, side, 1, pl.multiple_of(c0 + 2 * LANES, LANES))
            for m, step in enumerate(matrix):
                slots.setdefault(m * len(tiles) // len(matrix), []).append(step)
        for a in range(comp):
            slots.setdefault(a * len(tiles) // comp, []).append(functools.partial(tile_dot, a))
        for m, step in enumerate(extra):
            slots.setdefault(m * len(tiles) // len(extra), []).append(step)

        for m, (t, k0) in enumerate(tiles):
            for step in slots.get(m, []):
                step()
            at = pl.multiple_of(c0 + (t + 1) * LANES, LANES)
            values = []
            for b in range(comp):
                here = z[s, b, k0 : k0 + ROWS, pl.ds(at, LANES)]
                low = jnp.where(last, z[s, b, k0 : k0 + ROWS, pl.ds(at - LANES, LANES)], here)
                high = jnp.where(first, z[s, b, k0 : k0 + ROWS, pl.ds(at + LANES, LANES)], here)
                values.append(
                    (
                        here.astype(F32),
                        pltpu.roll(low.astype(F32), 1, 1),
                        pltpu.roll(high.astype(F32), LANES - 1, 1),
                    )
                )
            for a in range(comp):
                acc = None
                for b in range(comp):
                    for d in range(3):
                        weight = coef[d, a, b, side : side + 1, t * LANES : (t + 1) * LANES]
                        term = weight * values[b][d]
                        acc = term if acc is None else acc + term
                applied[side, a, k0 : k0 + ROWS, t * LANES : (t + 1) * LANES] = acc.astype(BF16)
        diag_ref[sp] += functools.reduce(lambda p, q: p + q, total)

    def weights(it):
        i = it // chunks
        c0 = pl.multiple_of(lax.rem(it, chunks) * WIDE, WIDE)
        for d in range(3):
            for a in range(comp):
                coef[d, a] = jac[d, i, a, :, :, pl.ds(c0, WIDE)].astype(F32)

    def with_faces(it, carry):
        @pl.when((lax.rem(it, 2) == 1) & (it < 8 * nx - 1))
        def _():
            for copy in loads((it + 1) // 2):
                copy.wait()

        i = it // 8
        fs = i * ny + lax.rem(it, 2)
        block = lax.rem(it, 8) // 2

        def piece(h):
            pair, k = h % 2, h // 2
            k0 = pl.multiple_of(block * quarter + k * PIECE, PIECE)
            wanted = jnp.concatenate(
                [cells_ref[fs, 2 * pair : 2 * pair + 1], cells_ref[fs, 2 * pair + 1 : 2 * pair + 2]], axis=1
            )
            near = jnp.broadcast_to(wanted - k0, (16, 2 * nface)).astype(jnp.int16)
            pick = jnp.concatenate(
                [jnp.where(place == near - 16 * r, one, nil) for r in range(PIECE // 16)], axis=0
            )
            part = jnp.dot(
                z[fs, :, :, pl.ds(pl.multiple_of(k0 + LANES, LANES), PIECE)].reshape(comp * kdim, PIECE),
                pick,
                preferred_element_type=F32,
            )
            if k == 0:
                gather[fs, pair] = part + jnp.where(block == 0, 0.0, gather[fs, pair])
            else:
                gather[fs, pair] += part

        steps = [functools.partial(piece, h) for h in range(2 * quarter // PIECE)]
        weights(it)
        stencil(it, 0, steps[:1], True)
        stencil(it, 1, steps[1:], False)
        return carry

    def without_faces(it, carry):
        weights(it)
        stencil(it, 0, [], True)
        stencil(it, 1, [], True)
        return carry

    small[0].wait()
    for copy in loads(0):
        copy.wait()
    for n in range(2, 4 * nx):
        for copy in loads(n):
            copy.start()

    def push(s, carry):
        for d in range(4):
            picked = []
            for b in range(comp):
                values = gather[s, d // 2, b * kdim : (b + 1) * kdim, (d % 2) * nface : (d % 2 + 1) * nface]
                faces[s, d, :, b * nface : (b + 1) * nface] = values.astype(BF16)
                picked.append(values)
            for a in range(comp):
                acc = None
                for b in range(comp):
                    term = couple_ref[s, a, b].astype(F32)[d : d + 1] * picked[b]
                    acc = term if acc is None else acc + term
                pushed[s, d, :, a * nface : (a + 1) * nface] = acc.astype(BF16)
        return carry

    def tile(s, e, right):
        return lax.dot_general(faces[s, e], right, NT, preferred_element_type=F32)

    steps_of = ((1, 0), (-1, 0), (0, 1), (0, -1))

    def sources(d):
        if d == 0:
            return [(nx - 1) * ny + j for j in range(ny)]
        if d == 1:
            return list(range(ny))
        if d == 2:
            return [i * ny + ny - 1 for i in range(nx)]
        return [i * ny for i in range(nx)]

    sends, start_of = [], []
    for d in range(4):
        for m, s in enumerate(sources(d)):
            start_of.append(s)
            sends.append(
                pltpu.make_async_remote_copy(
                    src_ref=pushed.at[s, d],
                    dst_ref=arrived.at[d, m],
                    send_sem=send_sem.at[d, m],
                    recv_sem=recv_sem.at[d, m],
                    device_id=neighbour_of(d),
                    device_id_type=MESH,
                )
            )
    for i in range(nx):
        lax.fori_loop(8 * i, 8 * (i + 1), with_faces, 0)
        if i == 0:
            small[1].wait()
            pl.semaphore_wait(barrier, 4)
        for s in range(i * ny, (i + 1) * ny):
            push(s, 0)
            for e in range(4):
                ti, tj = s // ny + steps_of[e][0], s % ny + steps_of[e][1]
                other = ti * ny + tj
                if 0 <= ti < nx and 0 <= tj < ny and other < s:
                    off_ref[s, e] = tile(s, e, pushed[other, OPPOSITE[e]])
                    off_ref[other, OPPOSITE[e]] = tile(other, OPPOSITE[e], pushed[s, e])
            for start, copy in zip(start_of, sends):
                if start == s:
                    copy.start()

    lax.fori_loop(8 * nx, nx * chunks, without_faces, 0)

    final = functools.reduce(
        lambda p, q: p + q,
        [
            lax.dot_general(
                applied[1, a], z[subs - 1, a, :, LANES + ncell - WIDE : LANES + ncell], NT,
                preferred_element_type=F32,
            )
            for a in range(comp)
        ],
    )
    diag_ref[subs - 1] += final
    for s in range(subs):
        diag_ref[s] = diag_ref[s].T

    for copy in sends:
        copy.wait()
    for e in range(4):
        d = OPPOSITE[e]
        inside = has_neighbour(e)
        for m, s in enumerate(sources(e)):
            off_ref[s, e] = jnp.where(inside, tile(s, e, arrived[d, m]), 0.0)


def hand_over(diag_in, off_in, diag_out, off_out, diag, off, sems):
    parts = [(diag_in, diag, diag_out)]
    parts += [(off_in.at[s], off.at[s], off_out.at[s]) for s in range(off_in.shape[0])]
    reads = [pltpu.make_async_copy(a, b, sems.at[0, n]) for n, (a, b, _) in enumerate(parts)]
    writes = [pltpu.make_async_copy(b, c, sems.at[1, n]) for n, (_, b, c) in enumerate(parts)]
    for copy in reads:
        copy.start()
    for read, write in zip(reads, writes):
        read.wait()
        write.start()
    for copy in writes:
        copy.wait()


def on_device(z_basis, jac_center, jac_lower, jac_upper, face_cells, couple):
    nx, ny, comp, kdim, ncell = z_basis.shape
    nface = face_cells.shape[-1]
    subs = nx * ny
    merge = lambda array: array.reshape((subs,) + array.shape[2:])
    paired = [jnp.transpose(array, (0, 2, 3, 1, 4)) for array in (jac_center, jac_lower, jac_upper)]
    wide = comp * nface
    shapes = (
        jax.ShapeDtypeStruct((subs, kdim, kdim), F32),
        jax.ShapeDtypeStruct((subs, 4, kdim, kdim), F32),
    )
    results = pl.pallas_call(
        functools.partial(kernel, (nx, ny, comp, kdim, ncell, nface)),
        out_shape=shapes,
        in_specs=[pl.BlockSpec(memory_space=pl.ANY)] * 6,
        out_specs=[pl.BlockSpec(memory_space=pltpu.VMEM)] * 2,
        scratch_shapes=[
            pltpu.VMEM((subs, comp, kdim, ncell + 2 * LANES), BF16),
            pltpu.VMEM((3, nx, comp, comp, ny, ncell), BF16),
            pltpu.VMEM((subs, 4, nface), jnp.int32),
            pltpu.VMEM((subs, comp, comp, 4, nface), BF16),
            pltpu.VMEM((3, comp, comp, ny, WIDE), F32),
            pltpu.VMEM((2, comp, kdim, WIDE), BF16),
            pltpu.VMEM((subs, 2, comp * kdim, 2 * nface), F32),
            pltpu.VMEM((subs, 4, kdim, wide), BF16),
            pltpu.VMEM((subs, 4, kdim, wide), BF16),
            pltpu.VMEM((4, 2, kdim, wide), BF16),
            pltpu.SemaphoreType.DMA((4 * nx, 3 + ny)),
            pltpu.SemaphoreType.DMA((2,)),
            pltpu.SemaphoreType.DMA((4, 2)),
            pltpu.SemaphoreType.DMA((4, 2)),
        ],
        compiler_params=pltpu.CompilerParams(
            collective_id=0, has_side_effects=True, vmem_limit_bytes=56 * 2**20
        ),
        cost_estimate=pl.CostEstimate(flops=10**10, bytes_accessed=17 * 10**6, transcendentals=0),
    )(
        merge(z_basis), *paired, merge(face_cells), merge(jnp.transpose(couple, (0, 1, 3, 4, 2, 5)))
    )
    diag, off = pl.pallas_call(
        hand_over,
        out_shape=shapes,
        in_specs=[pl.BlockSpec(memory_space=pl.ANY)] * 2,
        out_specs=[pl.BlockSpec(memory_space=pl.ANY)] * 2,
        scratch_shapes=[
            pltpu.VMEM(shapes[0].shape, F32),
            pltpu.VMEM(shapes[1].shape, F32),
            pltpu.SemaphoreType.DMA((2, 1 + subs)),
        ],
        compiler_params=pltpu.CompilerParams(vmem_limit_bytes=56 * 2**20),
    )(*results)
    return diag.reshape(nx, ny, kdim, kdim), off.reshape(nx, ny, 4, kdim, kdim)


def solution(mesh):
    in_specs = (
        P("sub", "col", None, None, None),
        P("sub", "col", None, None, None),
        P("sub", "col", None, None, None),
        P("sub", "col", None, None, None),
        P("sub", "col", None, None),
        P("sub", "col", None, None, None, None),
    )
    out_specs = (P("sub", "col", None, None), P("sub", "col", None, None, None))
    return jax.shard_map(
        on_device, mesh=mesh, in_specs=in_specs, out_specs=out_specs, check_vma=False
    )
```
